32 devices in a mesh: req: 8 (over z, y), tp: 4 (over x, core).
Axes of the slice: x: 2, y: 2, z: 4, core: 2. Of those that a mesh axis runs over, the one named last changes fastest.
Arguments:
- tokens: bfloat16 [128, 2048], P('req'), may hold values from -6 to 6
- lengths: int32 [128], P('req'), may hold values from 1 to 8192, 32768 in all
- pool_order: int32 [128], replicated, may hold values from 0 to 127, each once
- positions: int32 [128], P('req'), may hold values from 0 to 16383
- slot_mask: int32 [32768], P('req'), may hold values 0 or 1
- kv_cache: bfloat16 [32768, 2, 1024], P('req', None, 'tp'), may hold values from -420 to 420
- attn_gain: bfloat16 [2048], replicated, may hold values from 0.25 to 1.75
- w_query: bfloat16 [2048, 2048], P(None, 'tp'), may hold values from -0.125 to 0.125
- w_key: bfloat16 [2048, 1024], P(None, 'tp'), may hold values from -0.125 to 0.125
- w_value: bfloat16 [2048, 1024], P(None, 'tp'), may hold values from -0.125 to 0.125
- w_out: bfloat16 [2048, 2048], P('tp'), may hold values from -0.125 to 0.125
- ffn_gain: bfloat16 [2048], replicated, may hold values from 0.25 to 1.75
- w_gate: bfloat16 [2048, 4096], P(None, 'tp'), may hold values from -0.125 to 0.125
- w_up: bfloat16 [2048, 4096], P(None, 'tp'), may hold values from -0.125 to 0.125
- w_down: bfloat16 [4096, 2048], P('tp'), may hold values from -0.09375 to 0.09375
Outputs:
- hidden_out: float32 [128, 2048], P('req')
- new_kv: float32 [128, 2, 1024], P('req', None, 'tp')
The draws below stay inside these ranges and needn't reach their ends.
Inputs may be any that keep to these rules, and one draw needn't show every extreme that they name: The lengths add up to 32768, so the requests' caches fill the pool end to end; the largest is exactly 8192. `pool_order`: each request appears exactly once.
All inputs are finite; a program needn't handle non-finite values. No bound on the sum of `lengths` or of `slot_mask` on one device may be relied on, other than what follows from the above.
Results may differ from the reference program's by a relative error of at most 0.013.
The reference program's roundings to bfloat16 on the way count: a program that leaves them out, or rounds other values in their place, can miss the bound.
Values may be sent and summed in bfloat16 or wider, within the bound.
No kernel may reach another device: no remote copies, remote signals or barrier semaphores. Data moves between devices by JAX's collectives and lax.ppermute only.
A program may use at most 192 MiB of HBM per device.

```python
import math
import jax
import jax.numpy as jnp
import numpy as np
from jax import lax

D = 2048
HEADS = 16
KV_HEADS = 8
HEAD_DIM = 128
FF = 4096
MOST = 8192
REQS = 128
SLOT_DEV = 4096
SLOTS = 32768
N_REQ = 8


def draw_kv_cache(key, part):
    shape = (SLOTS, 2, KV_HEADS * HEAD_DIM)
    first = jax.random.fold_in(jax.random.fold_in(key, 17), 0)
    scales = jnp.array([1.5, 2.0], jnp.float32)[None, :, None]
    base = jnp.clip(jax.random.normal(first, shape, jnp.float32), -5.0, 5.0)
    return (base * scales).astype(jnp.bfloat16)


def touch_ends(result, own_key, low, top_value):
    extent = result.shape
    spot = [jax.random.randint(jax.random.fold_in(own_key, axis), (), 0, extent[axis]) for axis in range(len(extent))]
    result = result.at[tuple(spot)].set(low)
    longest = extent.index(max(extent))
    spot[longest] = (spot[longest] + 1) % extent[longest]
    return result.at[tuple(spot)].set(top_value)


def level_of(own_key, dims, cuts, least, largest):
    def one(position, shards_of):
        draws = jax.random.uniform(jax.random.fold_in(jax.random.fold_in(own_key, 6), position), (shards_of,), jnp.float32, least / len(cuts), largest / len(cuts))
        return jnp.repeat(jnp.exp(draws), dims[position] // shards_of).reshape((-1,) + (1,) * (len(dims) - position - 1))

    factor_of = one(*cuts[0])
    for cut in cuts[1:]:
        factor_of = factor_of * one(*cut)
    return factor_of


def length_profile(number_of, total, reach, skew):
    loads = [(1 << 20) // math.isqrt(grade ** skew) + 1 for grade in range(2, number_of + 1)]
    surplus, given = total - reach - (number_of - 1), [1] * (number_of - 1)
    while surplus > 0:
        free = [i for i in range(number_of - 1) if given[i] < reach]
        whole, remaining = sum([loads[i] for i in free]), surplus
        for i in free:
            addition = min(reach - given[i], max(1, remaining * loads[i] // whole), surplus)
            given[i] = given[i] + addition
            surplus = surplus - addition
    return np.array([reach] + given)


def uneven(stream_key, amount, total, reach, slope):
    if amount == 2:
        one = jax.random.randint(stream_key, (), max(1, total - reach), min(reach, total - 1) + 1)
        return jnp.stack([one, total - one])
    sizes = jnp.asarray(length_profile(amount, total, reach, slope), jnp.int32)
    pairs = (amount - 1) // 2
    source_of, receiver = sizes[1:1 + 2 * pairs:2], sizes[2:2 + 2 * pairs:2]
    margin = jnp.minimum(source_of - 1, reach - receiver)
    shifted = jax.random.randint(jax.random.fold_in(stream_key, 1), (pairs,), 0, 1 << 20) % (margin + 1)
    sizes = sizes.at[1:1 + 2 * pairs:2].set(source_of - shifted).at[2:2 + 2 * pairs:2].set(receiver + shifted)
    return sizes[jax.random.permutation(jax.random.fold_in(stream_key, 2), amount)]


def gaussian(stream_key, shape, deviation, reach, cuts=(), kind=jnp.bfloat16):
    values = jax.random.normal(stream_key, shape, jnp.float32) * deviation
    if len(cuts) > 0:
        values = level_of(stream_key, shape, cuts, -0.22, 0.18) * values
    return jnp.clip(values, min=-reach, max=reach).astype(kind)


def setup_inputs(seed: int = 0) -> dict:
    key_list = jax.random.split(jax.random.key(seed), 16)
    return {
        "tokens": gaussian(key_list[0], (REQS, D), 1.0, 6.0, ((0, 8),)),
        "lengths": uneven(key_list[1], REQS, SLOTS, MOST, 2).astype(jnp.int32),
        "pool_order": jax.random.permutation(key_list[2], REQS).astype(jnp.int32),
        "positions": touch_ends(jax.random.randint(key_list[3], (REQS,), 0, 16384), jax.random.fold_in(key_list[3], 1), 0, 16383).astype(jnp.int32),
        "slot_mask": touch_ends((jax.random.randint(key_list[4], (SLOTS,), 0, 8) < 7).astype(jnp.int32), jax.random.fold_in(key_list[4], 1), 0, 1),
        "kv_cache": draw_kv_cache(jax.random.fold_in(key_list[15], 71), 0),
        "attn_gain": jnp.clip(1.0 + 0.15 * jax.random.normal(key_list[6], (D,), jnp.float32), 0.25, 1.75).astype(jnp.bfloat16),
        "w_query": gaussian(key_list[7], (D, HEADS * HEAD_DIM), D ** -0.5, 0.125, ((1, 4),)),
        "w_key": gaussian(key_list[8], (D, KV_HEADS * HEAD_DIM), D ** -0.5, 0.125, ((1, 4),)),
        "w_value": gaussian(key_list[9], (D, KV_HEADS * HEAD_DIM), D ** -0.5, 0.125, ((1, 4),)),
        "w_out": gaussian(key_list[10], (HEADS * HEAD_DIM, D), (HEADS * HEAD_DIM) ** -0.5, 0.125, ((0, 4),)),
        "ffn_gain": jnp.clip(1.0 + 0.15 * jax.random.normal(key_list[11], (D,), jnp.float32), 0.25, 1.75).astype(jnp.bfloat16),
        "w_gate": gaussian(key_list[12], (D, FF), D ** -0.5, 0.125, ((1, 4),)),
        "w_up": gaussian(key_list[13], (D, FF), D ** -0.5, 0.125, ((1, 4),)),
        "w_down": gaussian(key_list[14], (FF, D), FF ** -0.5, 0.09375, ((0, 4),)),
    }


ROPE_BASE = 1000000.0
EPS = 1e-05
FLOOR = -1e+30

def rms_norm(rows, gain):
    mean_sq = lax.optimization_barrier(jnp.mean(rows * rows, axis=-1, keepdims=True))
    return rows * lax.rsqrt(mean_sq + EPS) * gain.astype(jnp.float32)

def rotate(vectors, places):
    width = vectors.shape[-1]
    half = width // 2
    freq = ROPE_BASE ** (-(jnp.arange(half, dtype=jnp.float32) * 2.0) / width)
    angle = places.astype(jnp.float32)[:, None] * freq[None, :]
    cosine = jnp.cos(angle)[:, None, :]
    sine = jnp.sin(angle)[:, None, :]
    first = vectors[..., :half]
    second = vectors[..., half:]
    return jnp.concatenate([first * cosine - second * sine, second * cosine + first * sine], axis=-1)

def reference(tokens, lengths, pool_order, positions, slot_mask, kv_cache, attn_gain, w_query, w_key, w_value, w_out, ffn_gain, w_gate, w_up, w_down):
    group = HEADS // KV_HEADS
    scale = 1.0 / math.sqrt(HEAD_DIM)
    rows = tokens.astype(jnp.float32)
    normed = rms_norm(rows, attn_gain).astype(jnp.bfloat16)
    query = rotate(jnp.dot(normed, w_query, preferred_element_type=jnp.float32).reshape(REQS, HEADS, HEAD_DIM), positions).astype(jnp.bfloat16)
    key_full = rotate(jnp.dot(normed, w_key, preferred_element_type=jnp.float32).reshape(REQS, KV_HEADS, HEAD_DIM), positions)
    value_full = jnp.dot(normed, w_value, preferred_element_type=jnp.float32)
    new_kv = jnp.stack([key_full.reshape(REQS, KV_HEADS * HEAD_DIM), value_full], axis=1)
    new_key = key_full.astype(jnp.bfloat16)
    new_value = value_full.astype(jnp.bfloat16)
    ordered = lengths[pool_order]
    ends = jnp.cumsum(ordered).astype(jnp.int32)
    place = jnp.searchsorted(ends, jnp.arange(SLOTS, dtype=jnp.int32), side='right').astype(jnp.int32)
    owner = pool_order[place].astype(jnp.int32)
    grouped = query.reshape(REQS, KV_HEADS, group, HEAD_DIM)

    def block_scores(index):
        low = (index * SLOT_DEV).astype(jnp.int32)
        owners = lax.dynamic_slice_in_dim(owner, low, SLOT_DEV, 0)
        keys = lax.dynamic_slice_in_dim(kv_cache, low, SLOT_DEV, 0)[:, 0, :].reshape(SLOT_DEV, KV_HEADS, HEAD_DIM)
        return jnp.einsum('skgd,skd->skg', grouped[owners].astype(jnp.float32), keys.astype(jnp.float32)) * scale
    scores = lax.map(block_scores, jnp.arange(N_REQ, dtype=jnp.int32)).reshape(SLOTS, KV_HEADS, group)
    live = (slot_mask == 1)[:, None, None]
    scores = jnp.where(live, scores, FLOOR)
    cache_peak = jnp.full((REQS, KV_HEADS, group), FLOOR, jnp.float32).at[owner].max(scores)
    own_score = jnp.einsum('nkgd,nkd->nkg', grouped.astype(jnp.float32), new_key.astype(jnp.float32)) * scale
    peak = jnp.maximum(cache_peak, own_score)
    weights = jnp.where(live, jnp.exp(scores - peak[owner]), 0.0)
    own_weight = jnp.exp(own_score - peak)
    total = jax.ops.segment_sum(weights, owner, num_segments=REQS) + own_weight

    def add_block(carry, index):
        low = (index * SLOT_DEV).astype(jnp.int32)
        owners = lax.dynamic_slice_in_dim(owner, low, SLOT_DEV, 0)
        part = lax.dynamic_slice_in_dim(weights, low, SLOT_DEV, 0)
        values = lax.dynamic_slice_in_dim(kv_cache, low, SLOT_DEV, 0)[:, 1, :].reshape(SLOT_DEV, KV_HEADS, HEAD_DIM)
        term = part[..., None] * values[:, :, None, :].astype(jnp.float32)
        return (carry + jax.ops.segment_sum(term, owners, num_segments=REQS), None)
    summed, _ = lax.scan(add_block, jnp.zeros((REQS, KV_HEADS, group, HEAD_DIM), jnp.float32), jnp.arange(N_REQ, dtype=jnp.int32))
    summed = summed + own_weight[..., None] * new_value.reshape(REQS, KV_HEADS, 1, HEAD_DIM).astype(jnp.float32)
    context = (summed / total[..., None]).reshape(REQS, HEADS * HEAD_DIM).astype(jnp.bfloat16)
    mid = rows + jnp.dot(context, w_out, preferred_element_type=jnp.float32)
    normed_mid = rms_norm(mid, ffn_gain).astype(jnp.bfloat16)
    gate = jnp.dot(normed_mid, w_gate, preferred_element_type=jnp.float32)
    upper = jnp.dot(normed_mid, w_up, preferred_element_type=jnp.float32)
    act = (jax.nn.silu(gate) * upper).astype(jnp.bfloat16)
    hidden_out = mid + jnp.dot(act, w_down, preferred_element_type=jnp.float32)
    return (hidden_out, new_kv)
```

```python
import math

import jax
import jax.numpy as jnp
from jax import lax
from jax.experimental import pallas as pl
from jax.experimental.pallas import tpu as pltpu
from jax.sharding import PartitionSpec as P

HEAD_DIM = 128
ROPE_BASE = 1000000.0
EPS = 1e-05
FLOOR = -1e30
LOWEST = -1e29
LOG2E = 1.4426950408889634
TILE = 256
SUB = 128
WIN = 8
F32 = jnp.float32
BF16 = jnp.bfloat16
VMEM = pltpu.VMEM


def mm(a, b, dims=((1,), (0,))):
    return lax.dot_general(a, b, (dims, ((), ())), preferred_element_type=F32)


def norm_rows(rows, gain):
    mean_sq = jnp.mean(rows * rows, axis=-1, keepdims=True)
    return (rows * lax.rsqrt(mean_sq + EPS) * gain.astype(F32)).astype(BF16)


def project_kernel(tokens_ref, gain_ref, cos_ref, sin_ref, len_ref, wq_ref, wk_ref, wv_ref, msg_ref, kv_ref):
    normed = norm_rows(tokens_ref[...].astype(F32), gain_ref[...])
    cosine = cos_ref[...]
    sine = sin_ref[...]

    def rope(x):
        return x * cosine + pltpu.roll(x, HEAD_DIM // 2, 1) * sine

    q = mm(normed, wq_ref[...])
    width = q.shape[1]
    for low in range(0, width, HEAD_DIM):
        msg_ref[:, low : low + HEAD_DIM] = rope(q[:, low : low + HEAD_DIM]).astype(BF16)
    msg_ref[:, width:] = len_ref[...]
    k = mm(normed, wk_ref[...])
    half = k.shape[1]
    for low in range(0, half, HEAD_DIM):
        kv_ref[:, low : low + HEAD_DIM] = rope(k[:, low : low + HEAD_DIM])
    kv_ref[:, half:] = mm(normed, wv_ref[...])


def attend_kernel(
    base_ref, msg_ref, order_ref, live_ref, cache_ref, out_ref,
    queries, starts, ends, slots, top, total, summed, ranks, ranks_s, sem,
):
    reqs = msg_ref.shape[0]
    width = msg_ref.shape[1] - HEAD_DIM
    heads = width // HEAD_DIM
    kv_heads = slots.shape[0]
    group = heads // kv_heads
    per_slot = 2 * kv_heads
    tiles = cache_ref.shape[0] // (per_slot * TILE)
    span = TILE * per_slot
    sub_lanes = SUB * per_slot
    factor = LOG2E / math.sqrt(HEAD_DIM)
    base = base_ref[0].astype(F32)

    row = lax.broadcasted_iota(jnp.int32, (reqs, reqs), 0)
    col = lax.broadcasted_iota(jnp.int32, (reqs, reqs), 1)
    place = (order_ref[...] == row).astype(F32).astype(BF16)
    msg = msg_ref[...]
    sorted_msg = mm(place, msg, ((0,), (0,)))
    for h in range(heads):
        queries[h, 0:reqs, :] = sorted_msg[:, h * HEAD_DIM : (h + 1) * HEAD_DIM]
        queries[h, reqs:, :] = jnp.zeros((WIN, HEAD_DIM), F32)
    parts = sorted_msg[:, width:].astype(BF16)
    lane = lax.broadcasted_iota(jnp.int32, (reqs, HEAD_DIM), 1)
    high_half = lane < HEAD_DIM // 2

    def joined(counts):
        turned = pltpu.roll(counts, HEAD_DIM // 2, 1)
        return jnp.where(high_half, 128.0 * counts + turned, counts + 128.0 * turned)

    upto = joined(mm((col <= row).astype(F32).astype(BF16), parts)) - base
    before = joined(mm((col < row).astype(F32).astype(BF16), parts)) - base
    far = jnp.full((WIN, HEAD_DIM), 1e9, F32)
    ends[0:reqs, :] = upto
    ends[reqs:, :] = far
    starts[0:reqs, :] = before
    starts[reqs:, :] = far
    edge = (lane * TILE).astype(F32)
    first = jnp.sum((upto <= edge).astype(F32), axis=0, keepdims=True)
    last = jnp.sum((upto <= edge + (TILE - 1)).astype(F32), axis=0, keepdims=True)
    ranks[0:1, :] = first.astype(jnp.int32)
    ranks[1:2, :] = last.astype(jnp.int32)
    copy = pltpu.make_async_copy(ranks, ranks_s, sem)
    copy.start()

    blocks = live_ref.shape[0]
    out_lane = lax.broadcasted_iota(jnp.int32, (SUB, sub_lanes), 1)
    in_row = lax.broadcasted_iota(jnp.int32, (SUB, sub_lanes), 0)
    widen = (out_lane // per_slot == in_row).astype(F32).astype(BF16)
    alive = mm((live_ref[...] == 1).astype(F32).astype(BF16), widen) > 0.5
    lane_b = lax.broadcasted_iota(jnp.int32, (blocks, sub_lanes), 1)
    row_b = lax.broadcasted_iota(jnp.int32, (blocks, sub_lanes), 0)
    slot = (row_b * SUB + lane_b // per_slot).astype(F32)
    for c in range(kv_heads):
        slots[c, :, :] = jnp.where(alive & (lane_b % per_slot == 2 * c), slot, -1e9)

    top[...] = jnp.full(top.shape, LOWEST, F32)
    total[...] = jnp.zeros(total.shape, F32)
    summed[...] = jnp.zeros(summed.shape, F32)
    copy.wait()

    def part(tile, rank):
        q = jnp.concatenate(
            [queries[h, pl.ds(rank, WIN), :] for h in range(heads)], axis=0
        ).astype(BF16)
        low = starts[pl.ds(rank, WIN), :][:, 0:1]
        high = ends[pl.ds(rank, WIN), :][:, 0:1]
        chunk = cache_ref[pl.ds(tile * span, span), :]
        scores = mm(q, chunk, ((1,), (1,)))
        masks = []
        for c in range(kv_heads):
            at = jnp.concatenate(
                [slots[c, pl.ds(tile * (TILE // SUB) + i, 1), :] for i in range(TILE // SUB)], axis=1
            )
            masks.append((at >= low) & (at < high))
        masked = jnp.concatenate(
            [
                jnp.where(masks[h // group], scores[h * WIN : (h + 1) * WIN, :] * factor, FLOOR)
                for h in range(heads)
            ],
            axis=0,
        )
        peak = jnp.maximum(jnp.max(masked, axis=1, keepdims=True), LOWEST)
        weight = jnp.exp2(masked - peak)
        count = jnp.sum(weight, axis=1, keepdims=True)
        moved = jnp.concatenate(
            [pltpu.roll(weight[:, i : i + HEAD_DIM], 1, 1) for i in range(0, span, HEAD_DIM)], axis=1
        ).astype(BF16)
        return peak, count, mm(moved, chunk)

    def merge(rank, found):
        peak, count, value = found
        for h in range(heads):
            at = (h, pl.ds(rank, WIN), slice(None))
            rows = slice(h * WIN, (h + 1) * WIN)
            old = top[at]
            new = jnp.maximum(old, peak[rows, :])
            left = jnp.exp2(old - new)
            right = jnp.exp2(peak[rows, :] - new)
            top[at] = new
            total[at] = total[at] * left + count[rows, :] * right
            summed[at] = summed[at] * left + value[rows, :] * right

    for low in range(0, tiles, 4):
        some = range(low, min(low + 4, tiles))
        found = [part(t, ranks_s[0, t]) for t in some]
        for t, got in zip(some, found):
            merge(ranks_s[0, t], got)

    def more(t, carry):
        begin = ranks_s[0, t]

        def again(i, inner):
            rank = begin + (i + 1) * WIN
            merge(rank, part(t, rank))
            return inner

        return lax.fori_loop(0, (ranks_s[1, t] - begin) // WIN, again, carry)

    lax.fori_loop(0, tiles, more, 0)

    columns = []
    extra = jnp.zeros((reqs, HEAD_DIM), F32)
    for h in range(heads):
        sums = total[h, 0:reqs, :]
        some = sums > 0.0
        safe = jnp.where(some, sums, 1.0)
        columns.append((summed[h, 0:reqs, :] / safe).astype(BF16))
        rest = jnp.where(some, top[h, 0:reqs, :] + jnp.log2(safe), LOWEST)
        for piece in range(3):
            coded = rest.astype(BF16).astype(F32)
            extra = jnp.where(lane == piece * heads + h, coded, extra)
            rest = rest - coded
    both = jnp.concatenate(columns + [extra.astype(BF16)], axis=1)
    out_ref[...] = mm(place, both).astype(BF16)


def output_kernel(parts_ref, msg_ref, kv_ref, w_ref, out_ref):
    sources, count, wide = parts_ref.shape
    width = wide - HEAD_DIM
    heads = width // HEAD_DIM
    half = kv_ref.shape[1] // 2
    group = heads // (half // HEAD_DIM)
    factor = LOG2E / math.sqrt(HEAD_DIM)
    levels = []
    for r in range(sources):
        e = parts_ref[r, :, width:].astype(F32)
        levels.append(
            e + (pltpu.roll(e, HEAD_DIM - heads, 1) + pltpu.roll(e, HEAD_DIM - 2 * heads, 1))
        )
    context = []
    for h in range(heads):
        at = slice(h * HEAD_DIM, (h + 1) * HEAD_DIM)
        low = (h // group) * HEAD_DIM
        key = kv_ref[:, low : low + HEAD_DIM].astype(BF16).astype(F32)
        value = kv_ref[:, half + low : half + low + HEAD_DIM].astype(BF16).astype(F32)
        own = jnp.sum(msg_ref[:, at].astype(F32) * key, axis=1, keepdims=True) * factor
        cols = [level[:, h : h + 1] for level in levels]
        peak = own
        for c in cols:
            peak = jnp.maximum(peak, c)
        weight = jnp.exp2(own - peak)
        denom = weight
        numer = weight * value
        for r in range(sources):
            weight = jnp.exp2(cols[r] - peak)
            denom = denom + weight
            numer = numer + weight * parts_ref[r, :, at].astype(F32)
        context.append((numer / denom).astype(BF16))
    out_ref[...] = mm(jnp.concatenate(context, axis=1), w_ref[...]).astype(BF16)


def feed_kernel(tokens_ref, here_ref, there_ref, gain_ref, wg_ref, wu_ref, wd_ref, part_ref, mid_ref):
    mid = tokens_ref[...].astype(F32) + (here_ref[...].astype(F32) + there_ref[...].astype(F32))
    mid_ref[...] = mid
    normed = norm_rows(mid, gain_ref[...])
    gate = mm(normed, wg_ref[...])
    upper = mm(normed, wu_ref[...])
    act = (gate / (1.0 + jnp.exp(-gate)) * upper).astype(BF16)
    part_ref[...] = mm(act, wd_ref[...]).astype(BF16)


def swap(x, axis, distance):
    return lax.ppermute(x, axis, [(i, i ^ distance) for i in range(lax.axis_size(axis))])


def pair_sum(x):
    size = lax.axis_size("tp")
    distance = 1
    while distance * 2 < size:
        x = (x.astype(F32) + swap(x, "tp", distance).astype(F32)).astype(BF16)
        distance *= 2
    return x, swap(x, "tp", distance)


def per_device(
    tokens, lengths, pool_order, positions, slot_mask, kv_cache, attn_gain,
    w_query, w_key, w_value, w_out, ffn_gain, w_gate, w_up, w_down,
):
    count, model = tokens.shape
    nreq = lax.axis_size("req")
    reqs = count * nreq
    slot_count = kv_cache.shape[0]
    width = w_query.shape[1]
    half = w_key.shape[1]
    kv_heads = half // HEAD_DIM
    wide = width + HEAD_DIM
    assert slot_count % TILE == 0 and slot_count // TILE <= HEAD_DIM

    index = jnp.arange(HEAD_DIM, dtype=jnp.int32)
    pair = (index % (HEAD_DIM // 2)).astype(F32)
    freq = ROPE_BASE ** (-(pair * 2.0) / HEAD_DIM)
    angle = positions.astype(F32)[:, None] * freq[None, :]
    cosine = jnp.cos(angle)
    sine = jnp.where(index < HEAD_DIM // 2, -1.0, 1.0)[None, :] * jnp.sin(angle)
    coded = jnp.where(
        index[None, :] < HEAD_DIM // 2, lengths[:, None] >> 7, lengths[:, None] & 127
    ).astype(BF16)

    msg, new_kv = pl.pallas_call(
        project_kernel,
        out_shape=(
            jax.ShapeDtypeStruct((count, wide), BF16),
            jax.ShapeDtypeStruct((count, 2 * half), F32),
        ),
        compiler_params=pltpu.CompilerParams(vmem_limit_bytes=16 << 20),
        name="project",
    )(tokens, attn_gain.reshape(1, model), cosine, sine, coded, w_query, w_key, w_value)

    everyone = lax.all_to_all(jnp.broadcast_to(msg, (nreq, count, wide)), "req", 0, 0)
    everyone = everyone.reshape(reqs, wide)

    cache = kv_cache.reshape(slot_count, 2, kv_heads, HEAD_DIM).transpose(0, 2, 1, 3)
    cache = cache.reshape(slot_count * 2 * kv_heads, HEAD_DIM)
    live = slot_mask.reshape(slot_count // SUB, SUB)
    base = (lax.axis_index("req") * slot_count).astype(jnp.int32).reshape(1)
    rows = reqs + WIN
    per_head = (width // HEAD_DIM, rows, HEAD_DIM)
    parts = pl.pallas_call(
        attend_kernel,
        out_shape=jax.ShapeDtypeStruct((reqs, wide), BF16),
        in_specs=[pl.BlockSpec(memory_space=pltpu.SMEM)] + [pl.BlockSpec(memory_space=VMEM)] * 4,
        out_specs=pl.BlockSpec(memory_space=VMEM),
        scratch_shapes=[
            VMEM(per_head, F32),
            VMEM((rows, HEAD_DIM), F32),
            VMEM((rows, HEAD_DIM), F32),
            VMEM((kv_heads, slot_count // SUB, SUB * 2 * kv_heads), F32),
            VMEM(per_head, F32),
            VMEM(per_head, F32),
            VMEM(per_head, F32),
            VMEM((8, HEAD_DIM), jnp.int32),
            pltpu.SMEM((8, HEAD_DIM), jnp.int32),
            pltpu.SemaphoreType.DMA,
        ],
        compiler_params=pltpu.CompilerParams(vmem_limit_bytes=24 << 20),
        name="attend",
    )(base, everyone, pool_order.reshape(1, reqs), live, cache)

    mine = lax.all_to_all(parts.reshape(nreq, count, wide), "req", 0, 0)

    partial_attn = pl.pallas_call(
        output_kernel,
        out_shape=jax.ShapeDtypeStruct((count, model), BF16),
        compiler_params=pltpu.CompilerParams(vmem_limit_bytes=16 << 20),
        name="output",
    )(mine, msg, new_kv, w_out)

    here, there = pair_sum(partial_attn)
    down_part, mid = pl.pallas_call(
        feed_kernel,
        out_shape=(
            jax.ShapeDtypeStruct((count, model), BF16),
            jax.ShapeDtypeStruct((count, model), F32),
        ),
        compiler_params=pltpu.CompilerParams(vmem_limit_bytes=20 << 20),
        name="feed",
    )(tokens, here, there, ffn_gain.reshape(1, model), w_gate, w_up, w_down)

    here, there = pair_sum(down_part)
    hidden_out = mid + (here.astype(F32) + there.astype(F32))
    return (hidden_out, new_kv.reshape(count, 2, half))


def solution(mesh):
    placed = (
        P("req", None),
        P("req"),
        P(),
        P("req"),
        P("req"),
        P("req", None, "tp"),
        P(),
        P(None, "tp"),
        P(None, "tp"),
        P(None, "tp"),
        P("tp", None),
        P(),
        P(None, "tp"),
        P(None, "tp"),
        P("tp", None),
    )
    return jax.shard_map(
        per_device,
        mesh=mesh,
        in_specs=placed,
        out_specs=(P("req", None), P("req", None, "tp")),
        check_vma=False,
    )
```

```python
import math

import jax
import jax.numpy as jnp
import numpy as np
from jax import lax
from jax.experimental import pallas as pl
from jax.experimental.pallas import tpu as pltpu
from jax.sharding import PartitionSpec as P

HEAD_DIM = 128
ROPE_BASE = 1000000.0
EPS = 1e-05
FLOOR = -1e30
LOWEST = -1e29
LOG2E = 1.4426950408889634
TILE = 256
SUB = 128
WIN = 8
PIECES = 4
SLAB = 1024
F32 = jnp.float32
BF16 = jnp.bfloat16
VMEM = pltpu.VMEM


def mm(a, b, dims=((1,), (0,))):
    return lax.dot_general(a, b, (dims, ((), ())), preferred_element_type=F32)


def norm_rows(rows, gain_ref):
    mean_sq = jnp.mean(rows * rows, axis=-1, keepdims=True)
    scaled = rows * lax.rsqrt(mean_sq + EPS)
    gain = gain_ref[...].astype(F32)
    blocks = [
        scaled[:, i * HEAD_DIM : (i + 1) * HEAD_DIM] * gain[i : i + 1, :] for i in range(gain.shape[0])
    ]
    return jnp.concatenate(blocks, axis=1).astype(BF16)


def column(row_ref, count):
    shape = (count, count)
    diagonal = lax.broadcasted_iota(jnp.int32, shape, 0) == lax.broadcasted_iota(jnp.int32, shape, 1)
    values = jnp.broadcast_to(row_ref[...].astype(F32), shape)
    return jnp.sum(jnp.where(diagonal, values, 0.0), axis=1, keepdims=True)


def fetch(pairs, sems):
    copies = [pltpu.make_async_copy(src, dst, sems.at[i]) for i, (src, dst) in enumerate(pairs)]
    for copy in copies:
        copy.start()
    return copies


def project_kernel(
    tokens_hbm, gain_hbm, place_hbm, len_hbm, freq_hbm, wq_hbm,
    msg_ref, normed_ref, cos_ref, sin_ref,
    tokens, gain, place, lens, freq, wq, sems,
):
    sources, count, wide = msg_ref.shape
    width = wide - HEAD_DIM
    rows = wq.shape[0] // PIECES
    small = [(tokens_hbm, tokens), (gain_hbm, gain), (place_hbm, place), (len_hbm, lens), (freq_hbm, freq)]
    slabs = [pl.ds(i * rows, rows) for i in range(PIECES)]
    copies = fetch(small + [(wq_hbm.at[at, :], wq.at[at, :]) for at in slabs], sems)
    for copy in copies[: len(small)]:
        copy.wait()
    normed = norm_rows(tokens[...].astype(F32), gain)
    normed_ref[...] = normed
    lane = lax.broadcasted_iota(jnp.int32, (count, HEAD_DIM), 1)
    angle = column(place, count) * freq[...]
    cosine = jnp.cos(angle)
    sine = jnp.where(lane < HEAD_DIM // 2, -1.0, 1.0) * jnp.sin(angle)
    cos_ref[...] = cosine
    sin_ref[...] = sine
    length = column(lens, count)
    high = jnp.floor(length * (1.0 / 128.0))
    coded = jnp.where(lane < HEAD_DIM // 2, high, length - 128.0 * high).astype(BF16)
    q = jnp.zeros((count, width), F32)
    for copy, at in zip(copies[len(small) :], slabs):
        copy.wait()
        q = q + mm(normed[:, at.start : at.start + rows], wq[at, :])
    parts = []
    for low in range(0, width, HEAD_DIM):
        x = q[:, low : low + HEAD_DIM]
        parts.append((x * cosine + pltpu.roll(x, HEAD_DIM // 2, 1) * sine).astype(BF16))
    msg = jnp.concatenate(parts + [coded], axis=1)
    for r in range(sources):
        msg_ref[r, :, :] = msg


def prepare_kernel(
    normed_ref, cos_ref, sin_ref, wk_hbm, wv_hbm, cache_hbm, wo_hbm,
    kv_ref, key_ref, value_ref, wo_ref,
    wk, wv, cache, wide, sems,
):
    half = wk.shape[1]
    slabs = cache.shape[0] // SLAB
    per_slot = 2 * half // HEAD_DIM
    spots = [pl.ds(i * SLAB, SLAB) for i in range(slabs)]
    wanted = [(cache_hbm.at[at, :], cache.at[at, :]) for at in spots]
    copies = fetch(wanted + [(wk_hbm, wk), (wv_hbm, wv), (wo_hbm, wo_ref)], sems)
    slots = SLAB // per_slot
    for i, at in enumerate(spots):
        copies[i].wait()
        wide[i % 2, :, :] = cache[at, :].astype(F32)
        for j in range(per_slot):
            rows = wide[i % 2, pl.ds(j, slots, stride=per_slot), :].astype(BF16)
            to = value_ref if j % 2 else key_ref
            to[i * slots : (i + 1) * slots, (j // 2) * HEAD_DIM : (j // 2 + 1) * HEAD_DIM] = rows
    normed = normed_ref[...]
    cosine = cos_ref[...]
    sine = sin_ref[...]
    copies[slabs].wait()
    k = mm(normed, wk[...])
    for low in range(0, half, HEAD_DIM):
        x = k[:, low : low + HEAD_DIM]
        kv_ref[:, low : low + HEAD_DIM] = x * cosine + pltpu.roll(x, HEAD_DIM // 2, 1) * sine
    copies[slabs + 1].wait()
    kv_ref[:, half:] = mm(normed, wv[...])
    copies[slabs + 2].wait()


def attend_kernel(
    base_ref, msg_ref, order_ref, live_ref, key_ref, value_ref, wg_hbm, wu_hbm,
    out_ref, wg_ref, wu_ref,
    queries, starts, ends, top, total, summed, held, weights, ranks, ranks_s, sem, load_sems,
):
    loads = fetch([(wg_hbm, wg_ref), (wu_hbm, wu_ref)], load_sems)
    reqs = msg_ref.shape[0]
    width = msg_ref.shape[1] - HEAD_DIM
    heads = width // HEAD_DIM
    group = heads // (key_ref.shape[1] // HEAD_DIM)
    tiles = key_ref.shape[0] // TILE
    factor = LOG2E / math.sqrt(HEAD_DIM)
    base = base_ref[0].astype(F32)

    row = lax.broadcasted_iota(jnp.int32, (reqs, reqs), 0)
    col = lax.broadcasted_iota(jnp.int32, (reqs, reqs), 1)
    place = (order_ref[...] == row).astype(F32).astype(BF16)
    parts = mm(place, msg_ref[:, width:], ((0,), (0,))).astype(BF16)
    lane = lax.broadcasted_iota(jnp.int32, (reqs, HEAD_DIM), 1)
    high_half = lane < HEAD_DIM // 2

    def joined(counts):
        turned = pltpu.roll(counts, HEAD_DIM // 2, 1)
        return jnp.where(high_half, 128.0 * counts + turned, counts + 128.0 * turned)

    upto = joined(mm((col <= row).astype(F32).astype(BF16), parts)) - base
    edge = (lane * TILE).astype(F32)
    first = jnp.sum((upto <= edge).astype(F32), axis=0, keepdims=True)
    last = jnp.sum((upto <= edge + (TILE - 1)).astype(F32), axis=0, keepdims=True)
    ranks[0:1, :] = first.astype(jnp.int32)
    ranks[1:2, :] = last.astype(jnp.int32)
    copy = pltpu.make_async_copy(ranks, ranks_s, sem)
    copy.start()
    far = jnp.full((WIN, HEAD_DIM), 1e9, F32)
    ends[0:reqs, :] = upto
    ends[reqs:, :] = far
    starts[0:reqs, :] = upto - joined(parts.astype(F32))
    starts[reqs:, :] = far
    sorted_q = mm(place, msg_ref[:, :width], ((0,), (0,)))
    for h in range(heads):
        queries[h, 0:reqs, :] = sorted_q[:, h * HEAD_DIM : (h + 1) * HEAD_DIM]
        queries[h, reqs:, :] = jnp.zeros((WIN, HEAD_DIM), F32)
    top[...] = jnp.full(top.shape, LOWEST, F32)
    total[...] = jnp.zeros(total.shape, F32)
    summed[...] = jnp.zeros(summed.shape, F32)
    copy.wait()

    def spot(h, rank):
        return (h, pl.ds(rank, WIN), slice(None))

    def of_head(x, h):
        return x[h * WIN : (h + 1) * WIN, :]

    def masked_scores(tile, rank):
        none = jnp.zeros((WIN, HEAD_DIM), BF16)
        lines = []
        for h in range(heads):
            q = queries[spot(h, rank)].astype(BF16)
            lines.append(
                jnp.concatenate([q if c == h // group else none for c in range(heads // group)], axis=1)
            )
        keys = key_ref[pl.ds(tile * TILE, TILE), :]
        scores = mm(jnp.concatenate(lines, axis=0), keys, ((1,), (1,))) * factor
        low = starts[pl.ds(rank, WIN), :]
        high = ends[pl.ds(rank, WIN), :]
        masks = []
        for i in range(TILE // SUB):
            block = tile * (TILE // SUB) + i
            at = (lax.broadcasted_iota(jnp.int32, (1, SUB), 1) + block * SUB).astype(F32)
            at = jnp.where(live_ref[pl.ds(block, 1), :] == 1, at, -1e9)
            masks.append((at >= low) & (at < high))
        mask = jnp.concatenate(masks, axis=1)
        return jnp.concatenate([jnp.where(mask, of_head(scores, h), FLOOR) for h in range(heads)], axis=0)

    def values_of(tile, weight):
        value = mm(weight, value_ref[pl.ds(tile * TILE, TILE), :])
        return [
            of_head(value, h)[:, (h // group) * HEAD_DIM : (h // group + 1) * HEAD_DIM] for h in range(heads)
        ]

    begins = [ranks_s[0, t] for t in range(tiles)]
    for t in range(tiles):
        held[t, :, :] = masked_scores(t, begins[t])
    peaks = [jnp.max(held[t, :, :], axis=1, keepdims=True) for t in range(tiles)]
    for t in range(tiles):
        for h in range(heads):
            at = spot(h, begins[t])
            top[at] = jnp.maximum(top[at], of_head(peaks[t], h))
    counts = []
    for t in range(tiles):
        peak = jnp.concatenate([top[spot(h, begins[t])] for h in range(heads)], axis=0)
        weight = jnp.exp2(held[t, :, :] - jnp.concatenate([peak] * (TILE // HEAD_DIM), axis=1))
        weights[t, :, :] = weight.astype(BF16)
        counts.append(jnp.sum(weight, axis=1, keepdims=True))
    found = [values_of(t, weights[t, :, :]) for t in range(tiles)]
    for t in range(tiles):
        for h in range(heads):
            at = spot(h, begins[t])
            total[at] = total[at] + of_head(counts[t], h)
            summed[at] = summed[at] + found[t][h]

    def more(t, carry):
        begin = ranks_s[0, t]

        def again(i, inner):
            rank = begin + (i + 1) * WIN
            masked = masked_scores(t, rank)
            peak = jnp.maximum(jnp.max(masked, axis=1, keepdims=True), LOWEST)
            weight = jnp.exp2(masked - peak)
            count = jnp.sum(weight, axis=1, keepdims=True)
            value = values_of(t, weight.astype(BF16))
            for h in range(heads):
                at = spot(h, rank)
                old = top[at]
                new = jnp.maximum(old, of_head(peak, h))
                left = jnp.exp2(old - new)
                right = jnp.exp2(of_head(peak, h) - new)
                top[at] = new
                total[at] = total[at] * left + of_head(count, h) * right
                summed[at] = summed[at] * left + value[h] * right
            return inner

        return lax.fori_loop(0, (ranks_s[1, t] - begin) // WIN, again, carry)

    lax.fori_loop(0, tiles, more, 0)

    columns = []
    extra = jnp.zeros((reqs, HEAD_DIM), F32)
    for h in range(heads):
        sums = total[h, 0:reqs, :]
        some = sums > 0.0
        safe = jnp.where(some, sums, 1.0)
        columns.append((summed[h, 0:reqs, :] / safe).astype(BF16))
        rest = jnp.where(some, top[h, 0:reqs, :] + jnp.log2(safe), LOWEST)
        for piece in range(3):
            coded = rest.astype(BF16).astype(F32)
            extra = jnp.where(lane == piece * heads + h, coded, extra)
            rest = rest - coded
    both = jnp.concatenate(columns + [extra.astype(BF16)], axis=1)
    out_ref[...] = mm(place, both).astype(BF16)
    for load in loads:
        load.wait()


def load_kernel(after_hbm, w_hbm, w_ref, sem):
    copy = pltpu.make_async_copy(w_hbm, w_ref, sem)
    copy.start()
    copy.wait()


def output_kernel(parts_ref, msg_ref, kv_ref, w_ref, out_ref):
    sources, count, wide = parts_ref.shape
    width = wide - HEAD_DIM
    heads = width // HEAD_DIM
    half = kv_ref.shape[1] // 2
    group = heads // (half // HEAD_DIM)
    factor = LOG2E / math.sqrt(HEAD_DIM)
    levels = []
    for r in range(sources):
        e = parts_ref[r, :, width:].astype(F32)
        levels.append(
            e + (pltpu.roll(e, HEAD_DIM - heads, 1) + pltpu.roll(e, HEAD_DIM - 2 * heads, 1))
        )
    context = []
    for h in range(heads):
        at = slice(h * HEAD_DIM, (h + 1) * HEAD_DIM)
        low = (h // group) * HEAD_DIM
        key = kv_ref[:, low : low + HEAD_DIM].astype(BF16).astype(F32)
        value = kv_ref[:, half + low : half + low + HEAD_DIM].astype(BF16).astype(F32)
        own = jnp.sum(msg_ref[0, :, at].astype(F32) * key, axis=1, keepdims=True) * factor
        cols = [level[:, h : h + 1] for level in levels]
        peak = own
        for c in cols:
            peak = jnp.maximum(peak, c)
        weight = jnp.exp2(own - peak)
        denom = weight
        numer = weight * value
        for r in range(sources):
            weight = jnp.exp2(cols[r] - peak)
            denom = denom + weight
            numer = numer + weight * parts_ref[r, :, at].astype(F32)
        context.append((numer / denom).astype(BF16))
    out_ref[...] = mm(jnp.concatenate(context, axis=1), w_ref[...]).astype(BF16)


def feed_kernel(tokens_ref, here_ref, there_ref, gain_ref, wg_ref, wu_ref, wd_ref, part_ref, mid_ref):
    mid = tokens_ref[...].astype(F32) + (here_ref[...].astype(F32) + there_ref[...].astype(F32))
    mid_ref[...] = mid
    normed = norm_rows(mid, gain_ref)
    gate = mm(normed, wg_ref[...])
    upper = mm(normed, wu_ref[...])
    act = (gate / (1.0 + jnp.exp(-gate)) * upper).astype(BF16)
    part_ref[...] = mm(act, wd_ref[...]).astype(BF16)


def swap(x, axis, distance):
    return lax.ppermute(x, axis, [(i, i ^ distance) for i in range(lax.axis_size(axis))])


def pair_sum(x):
    size = lax.axis_size("tp")
    distance = 1
    while distance * 2 < size:
        x = (x.astype(F32) + swap(x, "tp", distance).astype(F32)).astype(BF16)
        distance *= 2
    return x, swap(x, "tp", distance)


def in_hbm(x):
    return pltpu.with_memory_space_constraint(x, pltpu.HBM)


def in_vmem(x):
    return pltpu.with_memory_space_constraint(x, VMEM)


def per_device(
    tokens, lengths, pool_order, positions, slot_mask, kv_cache, attn_gain,
    w_query, w_key, w_value, w_out, ffn_gain, w_gate, w_up, w_down,
):
    count, model = tokens.shape
    nreq = lax.axis_size("req")
    reqs = count * nreq
    slot_count = kv_cache.shape[0]
    width = w_query.shape[1]
    half = w_key.shape[1]
    kv_heads = half // HEAD_DIM
    wide = width + HEAD_DIM
    assert slot_count % TILE == 0 and slot_count // TILE <= HEAD_DIM

    hbm_spec = pl.BlockSpec(memory_space=pltpu.HBM)
    vmem_spec = pl.BlockSpec(memory_space=VMEM)
    pair = np.arange(HEAD_DIM) % (HEAD_DIM // 2)
    freq = jnp.asarray((ROPE_BASE ** (-(pair * 2.0) / HEAD_DIM)).astype(np.float32)).reshape(1, HEAD_DIM)
    gain_shape = (model // HEAD_DIM, HEAD_DIM)

    msg, normed, cosine, sine = pl.pallas_call(
        project_kernel,
        out_shape=(
            jax.ShapeDtypeStruct((nreq, count, wide), BF16),
            VMEM((count, model), BF16),
            VMEM((count, HEAD_DIM), F32),
            VMEM((count, HEAD_DIM), F32),
        ),
        in_specs=[hbm_spec] * 6,
        out_specs=[vmem_spec] * 4,
        scratch_shapes=[
            VMEM((count, model), BF16),
            VMEM(gain_shape, BF16),
            VMEM((1, count), jnp.int32),
            VMEM((1, count), jnp.int32),
            VMEM((1, HEAD_DIM), F32),
            VMEM((model, width), BF16),
            pltpu.SemaphoreType.DMA((5 + PIECES,)),
        ],
        compiler_params=pltpu.CompilerParams(vmem_limit_bytes=4 << 20),
        cost_estimate=pl.CostEstimate(flops=2 * count * model * width, bytes_accessed=3 * model * width, transcendentals=0),
        name="project",
    )(
        in_hbm(tokens),
        in_hbm(attn_gain.reshape(gain_shape)),
        in_hbm(positions.reshape(1, count)),
        in_hbm(lengths.reshape(1, count)),
        in_hbm(freq),
        in_hbm(w_query),
    )

    everyone = lax.all_to_all(msg, "req", 0, 0).reshape(reqs, wide)

    cache = kv_cache.reshape(slot_count, 2, kv_heads, HEAD_DIM).transpose(0, 2, 1, 3)
    cache = cache.reshape(slot_count * 2 * kv_heads, HEAD_DIM)
    new_kv, keys, values, near_out = pl.pallas_call(
        prepare_kernel,
        out_shape=(
            VMEM((count, 2 * half), F32),
            VMEM((slot_count, half), BF16),
            VMEM((slot_count, half), BF16),
            VMEM(w_out.shape, BF16),
        ),
        in_specs=[vmem_spec] * 3 + [hbm_spec] * 4,
        out_specs=[vmem_spec] * 4,
        scratch_shapes=[
            VMEM((model, half), BF16),
            VMEM((model, half), BF16),
            VMEM(cache.shape, BF16),
            VMEM((2, SLAB, HEAD_DIM), F32),
            pltpu.SemaphoreType.DMA((cache.shape[0] // SLAB + 3,)),
        ],
        compiler_params=pltpu.CompilerParams(vmem_limit_bytes=9 << 20),
        cost_estimate=pl.CostEstimate(flops=4 * count * model * half, bytes_accessed=3 * cache.size, transcendentals=0),
        name="prepare",
    )(normed, cosine, sine, in_hbm(w_key), in_hbm(w_value), in_hbm(cache), in_hbm(w_out))

    live = slot_mask.reshape(slot_count // SUB, SUB)
    base = (lax.axis_index("req") * slot_count).astype(jnp.int32).reshape(1)
    rows = reqs + WIN
    heads = width // HEAD_DIM
    tiles = slot_count // TILE
    per_head = (heads, rows, HEAD_DIM)
    parts, near_gate, near_up = pl.pallas_call(
        attend_kernel,
        out_shape=(
            jax.ShapeDtypeStruct((reqs, wide), BF16),
            VMEM(w_gate.shape, BF16),
            VMEM(w_up.shape, BF16),
        ),
        in_specs=[pl.BlockSpec(memory_space=pltpu.SMEM)] + [vmem_spec] * 5 + [hbm_spec] * 2,
        out_specs=[vmem_spec] * 3,
        scratch_shapes=[
            VMEM(per_head, F32),
            VMEM((rows, HEAD_DIM), F32),
            VMEM((rows, HEAD_DIM), F32),
            VMEM(per_head, F32),
            VMEM(per_head, F32),
            VMEM(per_head, F32),
            VMEM((tiles, heads * WIN, TILE), F32),
            VMEM((tiles, heads * WIN, TILE), BF16),
            VMEM((8, HEAD_DIM), jnp.int32),
            pltpu.SMEM((8, HEAD_DIM), jnp.int32),
            pltpu.SemaphoreType.DMA,
            pltpu.SemaphoreType.DMA((2,)),
        ],
        compiler_params=pltpu.CompilerParams(vmem_limit_bytes=(2 + reqs // 32) << 20),
        cost_estimate=pl.CostEstimate(flops=1 << 30, bytes_accessed=8 << 20, transcendentals=0),
        name="attend",
    )(base, everyone, pool_order.reshape(1, reqs), live, keys, values, in_hbm(w_gate), in_hbm(w_up))

    mine = lax.all_to_all(parts.reshape(nreq, count, wide), "req", 0, 0)

    partial_attn = pl.pallas_call(
        output_kernel,
        out_shape=jax.ShapeDtypeStruct((count, model), BF16),
        compiler_params=pltpu.CompilerParams(vmem_limit_bytes=4 << 20),
        name="output",
    )(mine, msg, new_kv, near_out)

    here, there = pair_sum(partial_attn)
    near_down = pl.pallas_call(
        load_kernel,
        out_shape=VMEM(w_down.shape, BF16),
        in_specs=[pl.BlockSpec(memory_space=pl.ANY), hbm_spec],
        out_specs=vmem_spec,
        scratch_shapes=[pltpu.SemaphoreType.DMA],
        compiler_params=pltpu.CompilerParams(vmem_limit_bytes=1 << 20),
        cost_estimate=pl.CostEstimate(flops=0, bytes_accessed=2 * w_down.size, transcendentals=0),
        name="load",
    )(here, in_hbm(w_down))
    down_part, mid = pl.pallas_call(
        feed_kernel,
        out_shape=(
            jax.ShapeDtypeStruct((count, model), BF16),
            jax.ShapeDtypeStruct((count, model), F32),
        ),
        compiler_params=pltpu.CompilerParams(vmem_limit_bytes=6 << 20),
        name="feed",
    )(tokens, here, there, ffn_gain.reshape(gain_shape), near_gate, near_up, near_down)

    here, there = pair_sum(down_part)
    hidden_out = mid + (here.astype(F32) + there.astype(F32))
    return (hidden_out, new_kv.reshape(count, 2, half))


def solution(mesh):
    placed = (
        P("req", None),
        P("req"),
        P(),
        P("req"),
        P("req"),
        P("req", None, "tp"),
        P(),
        P(None, "tp"),
        P(None, "tp"),
        P(None, "tp"),
        P("tp", None),
        P(),
        P(None, "tp"),
        P(None, "tp"),
        P("tp", None),
    )
    return jax.shard_map(
        per_device,
        mesh=mesh,
        in_specs=placed,
        out_specs=(P("req", None), P("req", None, "tp")),
        check_vma=False,
    )
```

```python
import math

import jax
import jax.numpy as jnp
import numpy as np
from jax import lax
from jax.experimental import pallas as pl
from jax.experimental.pallas import tpu as pltpu
from jax.sharding import PartitionSpec as P

HEAD_DIM = 128
ROPE_BASE = 1000000.0
EPS = 1e-05
FLOOR = -1e30
LOWEST = -1e29
LOG2E = 1.4426950408889634
TILE = 256
SUB = 128
WIN = 8
PIECES = 4
SLAB = 1024
F32 = jnp.float32
BF16 = jnp.bfloat16
VMEM = pltpu.VMEM


def mm(a, b, dims=((1,), (0,))):
    return lax.dot_general(a, b, (dims, ((), ())), preferred_element_type=F32)


def norm_rows(rows, gain_ref):
    mean_sq = jnp.mean(rows * rows, axis=-1, keepdims=True)
    scaled = rows * lax.rsqrt(mean_sq + EPS)
    gain = gain_ref[...].astype(F32)
    blocks = [
        scaled[:, i * HEAD_DIM : (i + 1) * HEAD_DIM] * gain[i : i + 1, :] for i in range(gain.shape[0])
    ]
    return jnp.concatenate(blocks, axis=1).astype(BF16)


def column(row_ref, count):
    shape = (count, count)
    diagonal = lax.broadcasted_iota(jnp.int32, shape, 0) == lax.broadcasted_iota(jnp.int32, shape, 1)
    values = jnp.broadcast_to(row_ref[...].astype(F32), shape)
    return jnp.sum(jnp.where(diagonal, values, 0.0), axis=1, keepdims=True)


def fetch(pairs, sems):
    copies = [pltpu.make_async_copy(src, dst, sems.at[i]) for i, (src, dst) in enumerate(pairs)]
    for copy in copies:
        copy.start()
    return copies


def project_kernel(
    tokens_hbm, gain_hbm, place_hbm, len_hbm, freq_hbm, wq_hbm,
    msg_ref, mine_ref, normed_ref, cos_ref, sin_ref,
    tokens, gain, place, lens, freq, wq, sems,
):
    sources, count, wide = msg_ref.shape
    width = wide - HEAD_DIM
    rows = wq.shape[0] // PIECES
    small = [(tokens_hbm, tokens), (gain_hbm, gain), (place_hbm, place), (len_hbm, lens), (freq_hbm, freq)]
    slabs = [pl.ds(i * rows, rows) for i in range(PIECES)]
    copies = fetch(small + [(wq_hbm.at[at, :], wq.at[at, :]) for at in slabs], sems)
    for copy in copies[: len(small)]:
        copy.wait()
    normed = norm_rows(tokens[...].astype(F32), gain)
    normed_ref[...] = normed
    lane = lax.broadcasted_iota(jnp.int32, (count, HEAD_DIM), 1)
    angle = column(place, count) * freq[...]
    cosine = jnp.cos(angle)
    sine = jnp.where(lane < HEAD_DIM // 2, -1.0, 1.0) * jnp.sin(angle)
    cos_ref[...] = cosine
    sin_ref[...] = sine
    length = column(lens, count)
    high = jnp.floor(length * (1.0 / 128.0))
    coded = jnp.where(lane < HEAD_DIM // 2, high, length - 128.0 * high).astype(BF16)
    q = jnp.zeros((count, width), F32)
    for copy, at in zip(copies[len(small) :], slabs):
        copy.wait()
        q = q + mm(normed[:, at.start : at.start + rows], wq[at, :])
    parts = []
    for low in range(0, width, HEAD_DIM):
        x = q[:, low : low + HEAD_DIM]
        parts.append((x * cosine + pltpu.roll(x, HEAD_DIM // 2, 1) * sine).astype(BF16))
    msg = jnp.concatenate(parts + [coded], axis=1)
    mine_ref[...] = msg
    for r in range(sources):
        msg_ref[r, :, :] = msg


def prepare_kernel(
    normed_ref, cos_ref, sin_ref, wk_hbm, wv_hbm, cache_hbm,
    kv_ref, key_ref, near_ref, far_hbm,
    wk, wv, cache, wide, far, sems, out_sems,
):
    half = wk.shape[1]
    slabs = cache.shape[0] // SLAB
    per_slot = 2 * half // HEAD_DIM
    spots = [pl.ds(i * SLAB, SLAB) for i in range(slabs)]
    wanted = [(cache_hbm.at[at, :], cache.at[at, :]) for at in spots]
    copies = fetch([(wk_hbm, wk), (wv_hbm, wv)] + wanted, sems)
    normed = normed_ref[...]
    cosine = cos_ref[...]
    sine = sin_ref[...]
    copies.pop(0).wait()
    k = mm(normed, wk[...])
    for low in range(0, half, HEAD_DIM):
        x = k[:, low : low + HEAD_DIM]
        kv_ref[:, low : low + HEAD_DIM] = x * cosine + pltpu.roll(x, HEAD_DIM // 2, 1) * sine
    copies.pop(0).wait()
    kv_ref[:, half:] = mm(normed, wv[...])
    slots = SLAB // per_slot
    outs = []
    for i, at in enumerate(spots):
        copies[i].wait()
        wide[i % 2, :, :] = cache[at, :].astype(F32)
        for j in range(per_slot):
            rows = wide[i % 2, pl.ds(j, slots, stride=per_slot), :].astype(BF16)
            to, first = key_ref, i * slots
            if j % 2:
                to, first = (far, first) if i < slabs // 2 else (near_ref, first - far.shape[0])
            to[first : first + slots, (j // 2) * HEAD_DIM : (j // 2 + 1) * HEAD_DIM] = rows
        if i < slabs // 2 and i % 4 == 3:
            block = pl.ds((i - 3) * slots, 4 * slots)
            outs.append(pltpu.make_async_copy(far.at[block, :], far_hbm.at[block, :], out_sems.at[i // 4]))
            outs[-1].start()
    for out in outs:
        out.wait()


def attend_kernel(
    base_ref, msg_ref, order_ref, live_ref, key_ref, near_ref, far_hbm, wg_hbm,
    out_ref, wg_ref,
    queries, starts, ends, top, total, summed, held, weights, value_ref, ranks, ranks_s, sem, load_sems,
):
    middle = far_hbm.shape[0]
    loads = fetch(
        [
            (far_hbm, value_ref.at[pl.ds(0, middle), :]),
            (near_ref, value_ref.at[pl.ds(middle, middle), :]),
            (wg_hbm, wg_ref),
        ],
        load_sems,
    )
    reqs = msg_ref.shape[0]
    width = msg_ref.shape[1] - HEAD_DIM
    heads = width // HEAD_DIM
    group = heads // (key_ref.shape[1] // HEAD_DIM)
    tiles = key_ref.shape[0] // TILE
    factor = LOG2E / math.sqrt(HEAD_DIM)
    base = base_ref[0].astype(F32)

    row = lax.broadcasted_iota(jnp.int32, (reqs, reqs), 0)
    col = lax.broadcasted_iota(jnp.int32, (reqs, reqs), 1)
    place = (order_ref[...] == row).astype(F32).astype(BF16)
    parts = mm(place, msg_ref[:, width:], ((0,), (0,))).astype(BF16)
    lane = lax.broadcasted_iota(jnp.int32, (reqs, HEAD_DIM), 1)
    high_half = lane < HEAD_DIM // 2

    def joined(counts):
        turned = pltpu.roll(counts, HEAD_DIM // 2, 1)
        return jnp.where(high_half, 128.0 * counts + turned, counts + 128.0 * turned)

    upto = joined(mm((col <= row).astype(F32).astype(BF16), parts)) - base
    edge = (lane * TILE).astype(F32)
    first = jnp.sum((upto <= edge).astype(F32), axis=0, keepdims=True)
    last = jnp.sum((upto <= edge + (TILE - 1)).astype(F32), axis=0, keepdims=True)
    ranks[0:1, :] = first.astype(jnp.int32)
    ranks[1:2, :] = last.astype(jnp.int32)
    copy = pltpu.make_async_copy(ranks, ranks_s, sem)
    copy.start()
    far = jnp.full((WIN, HEAD_DIM), 1e9, F32)
    ends[0:reqs, :] = upto
    ends[reqs:, :] = far
    starts[0:reqs, :] = upto - joined(parts.astype(F32))
    starts[reqs:, :] = far
    sorted_q = mm(place, msg_ref[:, :width], ((0,), (0,)))
    for h in range(heads):
        queries[h, 0:reqs, :] = sorted_q[:, h * HEAD_DIM : (h + 1) * HEAD_DIM]
        queries[h, reqs:, :] = jnp.zeros((WIN, HEAD_DIM), F32)
    top[...] = jnp.full(top.shape, LOWEST, F32)
    total[...] = jnp.zeros(total.shape, F32)
    summed[...] = jnp.zeros(summed.shape, F32)
    copy.wait()

    def spot(h, rank):
        return (h, pl.ds(rank, WIN), slice(None))

    def of_head(x, h):
        return x[h * WIN : (h + 1) * WIN, :]

    def masked_scores(tile, rank):
        none = jnp.zeros((WIN, HEAD_DIM), BF16)
        lines = []
        for h in range(heads):
            q = queries[spot(h, rank)].astype(BF16)
            lines.append(
                jnp.concatenate([q if c == h // group else none for c in range(heads // group)], axis=1)
            )
        keys = key_ref[pl.ds(tile * TILE, TILE), :]
        scores = mm(jnp.concatenate(lines, axis=0), keys, ((1,), (1,))) * factor
        low = starts[pl.ds(rank, WIN), :]
        high = ends[pl.ds(rank, WIN), :]
        masks = []
        for i in range(TILE // SUB):
            block = tile * (TILE // SUB) + i
            at = (lax.broadcasted_iota(jnp.int32, (1, SUB), 1) + block * SUB).astype(F32)
            at = jnp.where(live_ref[pl.ds(block, 1), :] == 1, at, -1e9)
            masks.append((at >= low) & (at < high))
        mask = jnp.concatenate(masks, axis=1)
        return jnp.concatenate([jnp.where(mask, of_head(scores, h), FLOOR) for h in range(heads)], axis=0)

    def values_of(tile, weight):
        value = mm(weight, value_ref[pl.ds(tile * TILE, TILE), :])
        return [
            of_head(value, h)[:, (h // group) * HEAD_DIM : (h // group + 1) * HEAD_DIM] for h in range(heads)
        ]

    begins = [ranks_s[0, t] for t in range(tiles)]
    for t in range(tiles):
        held[t, :, :] = masked_scores(t, begins[t])
    peaks = [jnp.max(held[t, :, :], axis=1, keepdims=True) for t in range(tiles)]
    for t in range(tiles):
        for h in range(heads):
            at = spot(h, begins[t])
            top[at] = jnp.maximum(top[at], of_head(peaks[t], h))
    counts = []
    for t in range(tiles):
        peak = jnp.concatenate([top[spot(h, begins[t])] for h in range(heads)], axis=0)
        weight = jnp.exp2(held[t, :, :] - jnp.concatenate([peak] * (TILE // HEAD_DIM), axis=1))
        weights[t, :, :] = weight.astype(BF16)
        counts.append(jnp.sum(weight, axis=1, keepdims=True))
    loads[0].wait()
    loads[1].wait()
    found = [values_of(t, weights[t, :, :]) for t in range(tiles)]
    for t in range(tiles):
        for h in range(heads):
            at = spot(h, begins[t])
            total[at] = total[at] + of_head(counts[t], h)
            summed[at] = summed[at] + found[t][h]

    def more(t, carry):
        begin = ranks_s[0, t]

        def again(i, inner):
            rank = begin + (i + 1) * WIN
            masked = masked_scores(t, rank)
            peak = jnp.maximum(jnp.max(masked, axis=1, keepdims=True), LOWEST)
            weight = jnp.exp2(masked - peak)
            count = jnp.sum(weight, axis=1, keepdims=True)
            value = values_of(t, weight.astype(BF16))
            for h in range(heads):
                at = spot(h, rank)
                old = top[at]
                new = jnp.maximum(old, of_head(peak, h))
                left = jnp.exp2(old - new)
                right = jnp.exp2(of_head(peak, h) - new)
                top[at] = new
                total[at] = total[at] * left + of_head(count, h) * right
                summed[at] = summed[at] * left + value[h] * right
            return inner

        return lax.fori_loop(0, (ranks_s[1, t] - begin) // WIN, again, carry)

    lax.fori_loop(0, tiles, more, 0)

    columns = []
    extra = jnp.zeros((reqs, HEAD_DIM), F32)
    for h in range(heads):
        sums = total[h, 0:reqs, :]
        some = sums > 0.0
        safe = jnp.where(some, sums, 1.0)
        columns.append((summed[h, 0:reqs, :] / safe).astype(BF16))
        rest = jnp.where(some, top[h, 0:reqs, :] + jnp.log2(safe), LOWEST)
        for piece in range(3):
            coded = rest.astype(BF16).astype(F32)
            extra = jnp.where(lane == piece * heads + h, coded, extra)
            rest = rest - coded
    both = jnp.concatenate(columns + [extra.astype(BF16)], axis=1)
    out_ref[...] = mm(place, both).astype(BF16)
    loads[2].wait()


def load_kernel(after_hbm, w_hbm, w_ref, sem):
    copy = pltpu.make_async_copy(w_hbm, w_ref, sem)
    copy.start()
    copy.wait()


def output_kernel(parts_ref, msg_ref, kv_ref, w_ref, out_ref):
    sources, count, wide = parts_ref.shape
    width = wide - HEAD_DIM
    heads = width // HEAD_DIM
    half = kv_ref.shape[1] // 2
    group = heads // (half // HEAD_DIM)
    factor = LOG2E / math.sqrt(HEAD_DIM)
    levels = []
    for r in range(sources):
        e = parts_ref[r, :, width:].astype(F32)
        levels.append(
            e + (pltpu.roll(e, HEAD_DIM - heads, 1) + pltpu.roll(e, HEAD_DIM - 2 * heads, 1))
        )
    context = []
    for h in range(heads):
        at = slice(h * HEAD_DIM, (h + 1) * HEAD_DIM)
        low = (h // group) * HEAD_DIM
        key = kv_ref[:, low : low + HEAD_DIM].astype(BF16).astype(F32)
        value = kv_ref[:, half + low : half + low + HEAD_DIM].astype(BF16).astype(F32)
        own = jnp.sum(msg_ref[:, at].astype(F32) * key, axis=1, keepdims=True) * factor
        cols = [level[:, h : h + 1] for level in levels]
        peak = own
        for c in cols:
            peak = jnp.maximum(peak, c)
        weight = jnp.exp2(own - peak)
        denom = weight
        numer = weight * value
        for r in range(sources):
            weight = jnp.exp2(cols[r] - peak)
            denom = denom + weight
            numer = numer + weight * parts_ref[r, :, at].astype(F32)
        context.append((numer / denom).astype(BF16))
    out_ref[...] = mm(jnp.concatenate(context, axis=1), w_ref[...]).astype(BF16)


def feed_kernel(tokens_ref, here_ref, there_ref, gain_ref, wg_ref, wu_ref, wd_ref, part_ref, mid_ref):
    mid = tokens_ref[...].astype(F32) + (here_ref[...].astype(F32) + there_ref[...].astype(F32))
    mid_ref[...] = mid
    normed = norm_rows(mid, gain_ref)
    gate = mm(normed, wg_ref[...])
    upper = mm(normed, wu_ref[...])
    act = (gate / (1.0 + jnp.exp(-gate)) * upper).astype(BF16)
    part_ref[...] = mm(act, wd_ref[...]).astype(BF16)


def swap(x, axis, distance):
    return lax.ppermute(x, axis, [(i, i ^ distance) for i in range(lax.axis_size(axis))])


def pair_sum(x):
    size = lax.axis_size("tp")
    distance = 1
    while distance * 2 < size:
        x = (x.astype(F32) + swap(x, "tp", distance).astype(F32)).astype(BF16)
        distance *= 2
    return x, swap(x, "tp", distance)


def in_hbm(x):
    return pltpu.with_memory_space_constraint(x, pltpu.HBM)


def in_vmem(x):
    return pltpu.with_memory_space_constraint(x, VMEM)


def per_device(
    tokens, lengths, pool_order, positions, slot_mask, kv_cache, attn_gain,
    w_query, w_key, w_value, w_out, ffn_gain, w_gate, w_up, w_down,
):
    count, model = tokens.shape
    nreq = lax.axis_size("req")
    reqs = count * nreq
    slot_count = kv_cache.shape[0]
    width = w_query.shape[1]
    half = w_key.shape[1]
    kv_heads = half // HEAD_DIM
    wide = width + HEAD_DIM
    assert slot_count % TILE == 0 and slot_count // TILE <= HEAD_DIM

    hbm_spec = pl.BlockSpec(memory_space=pltpu.HBM)
    vmem_spec = pl.BlockSpec(memory_space=VMEM)
    pair = np.arange(HEAD_DIM) % (HEAD_DIM // 2)
    freq = jnp.asarray((ROPE_BASE ** (-(pair * 2.0) / HEAD_DIM)).astype(np.float32)).reshape(1, HEAD_DIM)
    gain_shape = (model // HEAD_DIM, HEAD_DIM)

    msg, mine, normed, cosine, sine = pl.pallas_call(
        project_kernel,
        out_shape=(
            VMEM((nreq, count, wide), BF16),
            VMEM((count, wide), BF16),
            VMEM((count, model), BF16),
            VMEM((count, HEAD_DIM), F32),
            VMEM((count, HEAD_DIM), F32),
        ),
        in_specs=[hbm_spec] * 6,
        out_specs=[vmem_spec] * 5,
        scratch_shapes=[
            VMEM((count, model), BF16),
            VMEM(gain_shape, BF16),
            VMEM((1, count), jnp.int32),
            VMEM((1, count), jnp.int32),
            VMEM((1, HEAD_DIM), F32),
            VMEM((model, width), BF16),
            pltpu.SemaphoreType.DMA((5 + PIECES,)),
        ],
        compiler_params=pltpu.CompilerParams(vmem_limit_bytes=4 << 20),
        cost_estimate=pl.CostEstimate(flops=2 * count * model * width, bytes_accessed=3 * model * width, transcendentals=0),
        name="project",
    )(
        in_hbm(tokens),
        in_hbm(attn_gain.reshape(gain_shape)),
        in_hbm(positions.reshape(1, count)),
        in_hbm(lengths.reshape(1, count)),
        in_hbm(freq),
        in_hbm(w_query),
    )

    everyone = lax.all_to_all(msg, "req", 0, 0).reshape(reqs, wide)

    cache = kv_cache.reshape(slot_count, 2, kv_heads, HEAD_DIM).transpose(0, 2, 1, 3)
    cache = cache.reshape(slot_count * 2 * kv_heads, HEAD_DIM)
    new_kv, keys, near, far = pl.pallas_call(
        prepare_kernel,
        out_shape=(
            VMEM((count, 2 * half), F32),
            VMEM((slot_count, half), BF16),
            VMEM((slot_count // 2, half), BF16),
            pltpu.HBM((slot_count // 2, half), BF16),
        ),
        in_specs=[vmem_spec] * 3 + [hbm_spec] * 3,
        out_specs=[vmem_spec, vmem_spec, vmem_spec, hbm_spec],
        scratch_shapes=[
            VMEM((model, half), BF16),
            VMEM((model, half), BF16),
            VMEM(cache.shape, BF16),
            VMEM((2, SLAB, HEAD_DIM), F32),
            VMEM((slot_count // 2, half), BF16),
            pltpu.SemaphoreType.DMA((cache.shape[0] // SLAB + 2,)),
            pltpu.SemaphoreType.DMA((cache.shape[0] // SLAB // 8,)),
        ],
        compiler_params=pltpu.CompilerParams(vmem_limit_bytes=12 << 20),
        cost_estimate=pl.CostEstimate(flops=4 * count * model * half, bytes_accessed=3 * cache.size, transcendentals=0),
        name="prepare",
    )(normed, cosine, sine, in_hbm(w_key), in_hbm(w_value), in_hbm(cache))

    live = slot_mask.reshape(slot_count // SUB, SUB)
    base = (lax.axis_index("req") * slot_count).astype(jnp.int32).reshape(1)
    rows = reqs + WIN
    heads = width // HEAD_DIM
    tiles = slot_count // TILE
    per_head = (heads, rows, HEAD_DIM)
    parts, near_gate = pl.pallas_call(
        attend_kernel,
        out_shape=(
            jax.ShapeDtypeStruct((reqs, wide), BF16),
            VMEM(w_gate.shape, BF16),
        ),
        in_specs=[pl.BlockSpec(memory_space=pltpu.SMEM)] + [vmem_spec] * 5 + [hbm_spec] * 2,
        out_specs=[vmem_spec] * 2,
        scratch_shapes=[
            VMEM(per_head, F32),
            VMEM((rows, HEAD_DIM), F32),
            VMEM((rows, HEAD_DIM), F32),
            VMEM(per_head, F32),
            VMEM(per_head, F32),
            VMEM(per_head, F32),
            VMEM((tiles, heads * WIN, TILE), F32),
            VMEM((tiles, heads * WIN, TILE), BF16),
            VMEM((slot_count, half), BF16),
            VMEM((8, HEAD_DIM), jnp.int32),
            pltpu.SMEM((8, HEAD_DIM), jnp.int32),
            pltpu.SemaphoreType.DMA,
            pltpu.SemaphoreType.DMA((3,)),
        ],
        compiler_params=pltpu.CompilerParams(vmem_limit_bytes=(4 + reqs // 32) << 20),
        cost_estimate=pl.CostEstimate(flops=1 << 30, bytes_accessed=8 << 20, transcendentals=0),
        name="attend",
    )(base, everyone, pool_order.reshape(1, reqs), live, keys, near, in_hbm(far), in_hbm(w_gate))

    found = lax.all_to_all(parts.reshape(nreq, count, wide), "req", 0, 0)

    partial_attn = pl.pallas_call(
        output_kernel,
        out_shape=jax.ShapeDtypeStruct((count, model), BF16),
        compiler_params=pltpu.CompilerParams(vmem_limit_bytes=4 << 20),
        name="output",
    )(found, mine, new_kv, w_out)

    here, there = pair_sum(partial_attn)
    near_down = pl.pallas_call(
        load_kernel,
        out_shape=VMEM(w_down.shape, BF16),
        in_specs=[pl.BlockSpec(memory_space=pl.ANY), hbm_spec],
        out_specs=vmem_spec,
        scratch_shapes=[pltpu.SemaphoreType.DMA],
        compiler_params=pltpu.CompilerParams(vmem_limit_bytes=1 << 20),
        cost_estimate=pl.CostEstimate(flops=0, bytes_accessed=2 * w_down.size, transcendentals=0),
        name="load",
    )(here, in_hbm(w_down))
    down_part, mid = pl.pallas_call(
        feed_kernel,
        out_shape=(
            jax.ShapeDtypeStruct((count, model), BF16),
            jax.ShapeDtypeStruct((count, model), F32),
        ),
        compiler_params=pltpu.CompilerParams(vmem_limit_bytes=6 << 20),
        name="feed",
    )(tokens, here, there, ffn_gain.reshape(gain_shape), near_gate, w_up, near_down)

    here, there = pair_sum(down_part)
    hidden_out = mid + (here.astype(F32) + there.astype(F32))
    return (hidden_out, new_kv.reshape(count, 2, half))


def solution(mesh):
    placed = (
        P("req", None),
        P("req"),
        P(),
        P("req"),
        P("req"),
        P("req", None, "tp"),
        P(),
        P(None, "tp"),
        P(None, "tp"),
        P(None, "tp"),
        P("tp", None),
        P(),
        P(None, "tp"),
        P(None, "tp"),
        P("tp", None),
    )
    return jax.shard_map(
        per_device,
        mesh=mesh,
        in_specs=placed,
        out_specs=(P("req", None), P("req", None, "tp")),
        check_vma=False,
    )
```

```python
import math

import jax
import jax.numpy as jnp
import numpy as np
from jax import lax
from jax.experimental import pallas as pl
from jax.experimental.pallas import tpu as pltpu
from jax.sharding import PartitionSpec as P

HEAD_DIM = 128
ROPE_BASE = 1000000.0
EPS = 1e-05
FLOOR = -1e30
LOWEST = -1e29
LOG2E = 1.4426950408889634
TILE = 256
SUB = 128
WIN = 8
PIECES = 4
SLAB = 1024
F32 = jnp.float32
BF16 = jnp.bfloat16
VMEM = pltpu.VMEM


def mm(a, b, dims=((1,), (0,))):
    return lax.dot_general(a, b, (dims, ((), ())), preferred_element_type=F32)


def norm_rows(rows, gain_ref):
    mean_sq = jnp.mean(rows * rows, axis=-1, keepdims=True)
    scaled = rows * lax.rsqrt(mean_sq + EPS)
    gain = gain_ref[...].astype(F32)
    blocks = [
        scaled[:, i * HEAD_DIM : (i + 1) * HEAD_DIM] * gain[i : i + 1, :] for i in range(gain.shape[0])
    ]
    return jnp.concatenate(blocks, axis=1).astype(BF16)


def column(row_ref, count):
    shape = (count, count)
    diagonal = lax.broadcasted_iota(jnp.int32, shape, 0) == lax.broadcasted_iota(jnp.int32, shape, 1)
    values = jnp.broadcast_to(row_ref[...].astype(F32), shape)
    return jnp.sum(jnp.where(diagonal, values, 0.0), axis=1, keepdims=True)


def fetch(pairs, sems):
    copies = [pltpu.make_async_copy(src, dst, sems.at[i]) for i, (src, dst) in enumerate(pairs)]
    for copy in copies:
        copy.start()
    return copies


def project_kernel(
    tokens_hbm, gain_hbm, place_hbm, len_hbm, freq_hbm, order_hbm, wq_hbm,
    msg_ref, mine_ref, normed_hbm, turn_hbm, sort_hbm, upto_hbm, back_hbm,
    tokens, gain, place, lens, freq, order, wq, normed_ref, turn, sort_ref, upto_ref, back_ref, sems, out_sems,
):
    sources, count, wide = msg_ref.shape
    width = wide - HEAD_DIM
    rows = wq.shape[0] // PIECES
    small = [(tokens_hbm, tokens), (gain_hbm, gain), (place_hbm, place), (len_hbm, lens)]
    small += [(freq_hbm, freq), (order_hbm, order)]
    slabs = [pl.ds(i * rows, rows) for i in range(PIECES)]
    copies = fetch(small + [(wq_hbm.at[at, :], wq.at[at, :]) for at in slabs], sems)
    for copy in copies[: len(small)]:
        copy.wait()
    normed = norm_rows(tokens[...].astype(F32), gain)
    normed_ref[...] = normed
    lane = lax.broadcasted_iota(jnp.int32, (count, HEAD_DIM), 1)
    angle = column(place, count) * freq[...]
    cosine = jnp.cos(angle)
    sine = jnp.where(lane < HEAD_DIM // 2, -1.0, 1.0) * jnp.sin(angle)
    turn[0:count, :] = cosine
    turn[count:, :] = sine
    length = column(lens, count)
    high = jnp.floor(length * (1.0 / 128.0))
    coded = jnp.where(lane < HEAD_DIM // 2, high, length - 128.0 * high).astype(BF16)
    reqs = order.shape[1]
    row = lax.broadcasted_iota(jnp.int32, (reqs, reqs), 0)
    col = lax.broadcasted_iota(jnp.int32, (reqs, reqs), 1)
    sort = (column(order, reqs) == col.astype(F32)).astype(F32)
    sort_ref[...] = sort.astype(BF16)
    rank = jnp.sum(sort * row.astype(F32), axis=0, keepdims=True)
    upto_ref[...] = (rank <= row.astype(F32)).astype(F32).astype(BF16)
    back_ref[...] = (order[...] == row).astype(F32).astype(BF16)
    early = [(normed_ref, normed_hbm), (turn, turn_hbm), (sort_ref, sort_hbm), (upto_ref, upto_hbm), (back_ref, back_hbm)]
    outs = fetch(early, out_sems)
    q = jnp.zeros((count, width), F32)
    for copy, at in zip(copies[len(small) :], slabs):
        copy.wait()
        q = q + mm(normed[:, at.start : at.start + rows], wq[at, :])
    parts = []
    for low in range(0, width, HEAD_DIM):
        x = q[:, low : low + HEAD_DIM]
        parts.append((x * cosine + pltpu.roll(x, HEAD_DIM // 2, 1) * sine).astype(BF16))
    msg = jnp.concatenate(parts + [coded], axis=1)
    mine_ref[...] = msg
    for r in range(sources):
        msg_ref[r, :, :] = msg
    for out in outs:
        out.wait()


def prepare_kernel(
    normed_hbm, turn_hbm, wk_hbm, wv_hbm, cache_hbm,
    kv_ref, key_ref, near_ref, far_hbm,
    normed_ref, turn, wk, wv, cache, wide, far, sems, out_sems,
):
    half = wk.shape[1]
    slabs = cache.shape[0] // SLAB
    per_slot = 2 * half // HEAD_DIM
    spots = [pl.ds(i * SLAB, SLAB) for i in range(slabs)]
    wanted = [(cache_hbm.at[at, :], cache.at[at, :]) for at in spots]
    copies = fetch([(normed_hbm, normed_ref), (turn_hbm, turn), (wk_hbm, wk), (wv_hbm, wv)] + wanted, sems)
    for _ in range(3):
        copies.pop(0).wait()
    normed = normed_ref[...]
    cosine = turn[0 : turn.shape[0] // 2, :]
    sine = turn[turn.shape[0] // 2 :, :]
    k = mm(normed, wk[...])
    for low in range(0, half, HEAD_DIM):
        x = k[:, low : low + HEAD_DIM]
        kv_ref[:, low : low + HEAD_DIM] = x * cosine + pltpu.roll(x, HEAD_DIM // 2, 1) * sine
    copies.pop(0).wait()
    kv_ref[:, half:] = mm(normed, wv[...])
    slots = SLAB // per_slot
    outs = []
    for i, at in enumerate(spots):
        copies[i].wait()
        wide[i % 2, :, :] = cache[at, :].astype(F32)
        for j in range(per_slot):
            rows = wide[i % 2, pl.ds(j, slots, stride=per_slot), :].astype(BF16)
            to, first = key_ref, i * slots
            if j % 2:
                to, first = (far, first) if i < slabs // 2 else (near_ref, first - far.shape[0])
            to[first : first + slots, (j // 2) * HEAD_DIM : (j // 2 + 1) * HEAD_DIM] = rows
        if i < slabs // 2 and i % 4 == 3:
            block = pl.ds((i - 3) * slots, 4 * slots)
            outs.append(pltpu.make_async_copy(far.at[block, :], far_hbm.at[block, :], out_sems.at[i // 4]))
            outs[-1].start()
    for out in outs:
        out.wait()


def attend_kernel(
    base_ref, msg_ref, sort_ref, upto_ref, back_ref, live_ref, key_ref, near_ref, far_hbm, later_hbm,
    out_ref,
    queries, starts, ends, top, total, summed, held, weights, value_ref, ranks, ranks_s, sem, load_sems,
):
    middle = far_hbm.shape[0]
    loads = fetch(
        [
            (far_hbm, value_ref.at[pl.ds(0, middle), :]),
            (near_ref, value_ref.at[pl.ds(middle, middle), :]),
        ],
        load_sems,
    )
    reqs = msg_ref.shape[0]
    width = msg_ref.shape[1] - HEAD_DIM
    heads = width // HEAD_DIM
    group = heads // (key_ref.shape[1] // HEAD_DIM)
    tiles = key_ref.shape[0] // TILE
    factor = LOG2E / math.sqrt(HEAD_DIM)
    base = base_ref[0].astype(F32)

    lane = lax.broadcasted_iota(jnp.int32, (reqs, HEAD_DIM), 1)
    high_half = lane < HEAD_DIM // 2

    def joined(counts):
        turned = pltpu.roll(counts, HEAD_DIM // 2, 1)
        return jnp.where(high_half, 128.0 * counts + turned, counts + 128.0 * turned)

    upto = joined(mm(upto_ref[...], msg_ref[:, width:])) - base
    edge = (lane * TILE).astype(F32)
    first = jnp.sum((upto <= edge).astype(F32), axis=0, keepdims=True).astype(jnp.int32)
    last = jnp.sum((upto <= edge + (TILE - 1)).astype(F32), axis=0, keepdims=True).astype(jnp.int32)
    begins = [first[0, t] for t in range(tiles)]
    widest = jnp.max(jnp.where(lane[0:1, :] < tiles, last - first, 0))
    ranks[0:1, :] = first
    ranks[1:2, :] = last
    copy = pltpu.make_async_copy(ranks, ranks_s, sem)
    copy.start()
    sorted_msg = mm(sort_ref[...], msg_ref[...])
    far = jnp.full((WIN, HEAD_DIM), 1e9, F32)
    ends[0:reqs, :] = upto
    ends[reqs:, :] = far
    starts[0:reqs, :] = upto - joined(sorted_msg[:, width:])
    starts[reqs:, :] = far
    for h in range(heads):
        queries[h, 0:reqs, :] = sorted_msg[:, h * HEAD_DIM : (h + 1) * HEAD_DIM]
        queries[h, reqs:, :] = jnp.zeros((WIN, HEAD_DIM), F32)
    top[...] = jnp.full(top.shape, LOWEST, F32)
    total[...] = jnp.zeros(total.shape, F32)
    summed[...] = jnp.zeros(summed.shape, F32)

    def spot(h, rank):
        return (h, pl.ds(rank, WIN), slice(None))

    def of_head(x, h):
        return x[h * WIN : (h + 1) * WIN, :]

    def masked_scores(tile, rank):
        none = jnp.zeros((WIN, HEAD_DIM), BF16)
        lines = []
        for h in range(heads):
            q = queries[spot(h, rank)].astype(BF16)
            lines.append(
                jnp.concatenate([q if c == h // group else none for c in range(heads // group)], axis=1)
            )
        keys = key_ref[pl.ds(tile * TILE, TILE), :]
        scores = mm(jnp.concatenate(lines, axis=0), keys, ((1,), (1,))) * factor
        low = starts[pl.ds(rank, WIN), :]
        high = ends[pl.ds(rank, WIN), :]
        masks = []
        for i in range(TILE // SUB):
            block = tile * (TILE // SUB) + i
            at = (lax.broadcasted_iota(jnp.int32, (1, SUB), 1) + block * SUB).astype(F32)
            at = jnp.where(live_ref[pl.ds(block, 1), :] == 1, at, -1e9)
            masks.append((at >= low) & (at < high))
        mask = jnp.concatenate(masks, axis=1)
        return jnp.concatenate([jnp.where(mask, of_head(scores, h), FLOOR) for h in range(heads)], axis=0)

    def values_of(tile, weight):
        value = mm(weight, value_ref[pl.ds(tile * TILE, TILE), :])
        return [
            of_head(value, h)[:, (h // group) * HEAD_DIM : (h // group + 1) * HEAD_DIM] for h in range(heads)
        ]

    for t in range(tiles):
        held[t, :, :] = masked_scores(t, begins[t])
    peaks = [jnp.max(held[t, :, :], axis=1, keepdims=True) for t in range(tiles)]
    for t in range(tiles):
        for h in range(heads):
            at = spot(h, begins[t])
            top[at] = jnp.maximum(top[at], of_head(peaks[t], h))
    counts = []
    for t in range(tiles):
        peak = jnp.concatenate([top[spot(h, begins[t])] for h in range(heads)], axis=0)
        weight = jnp.exp2(held[t, :, :] - jnp.concatenate([peak] * (TILE // HEAD_DIM), axis=1))
        weights[t, :, :] = weight.astype(BF16)
        counts.append(jnp.sum(weight, axis=1, keepdims=True))
    loads[0].wait()
    loads[1].wait()
    found = [values_of(t, weights[t, :, :]) for t in range(tiles)]
    for t in range(tiles):
        for h in range(heads):
            at = spot(h, begins[t])
            total[at] = total[at] + of_head(counts[t], h)
            summed[at] = summed[at] + found[t][h]

    def more(t, carry):
        begin = ranks_s[0, t]

        def again(i, inner):
            rank = begin + (i + 1) * WIN
            masked = masked_scores(t, rank)
            peak = jnp.maximum(jnp.max(masked, axis=1, keepdims=True), LOWEST)
            weight = jnp.exp2(masked - peak)
            count = jnp.sum(weight, axis=1, keepdims=True)
            value = values_of(t, weight.astype(BF16))
            for h in range(heads):
                at = spot(h, rank)
                old = top[at]
                new = jnp.maximum(old, of_head(peak, h))
                left = jnp.exp2(old - new)
                right = jnp.exp2(of_head(peak, h) - new)
                top[at] = new
                total[at] = total[at] * left + of_head(count, h) * right
                summed[at] = summed[at] * left + value[h] * right
            return inner

        return lax.fori_loop(0, (ranks_s[1, t] - begin) // WIN, again, carry)

    copy.wait()

    @pl.when(widest >= WIN)
    def _():
        lax.fori_loop(0, tiles, more, 0)

    columns = []
    extra = jnp.zeros((reqs, HEAD_DIM), F32)
    for h in range(heads):
        sums = total[h, 0:reqs, :]
        some = sums > 0.0
        safe = jnp.where(some, sums, 1.0)
        columns.append((summed[h, 0:reqs, :] / safe).astype(BF16))
        rest = jnp.where(some, top[h, 0:reqs, :] + jnp.log2(safe), LOWEST)
        for piece in range(3):
            coded = rest.astype(BF16).astype(F32)
            extra = jnp.where(lane == piece * heads + h, coded, extra)
            rest = rest - coded
    both = jnp.concatenate(columns + [extra.astype(BF16)], axis=1)
    out_ref[...] = mm(back_ref[...], both).astype(BF16)


def output_kernel(parts_ref, msg_ref, kv_ref, w_ref, *rest):
    out_ref = rest[-1]
    sources, count, wide = parts_ref.shape
    width = wide - HEAD_DIM
    heads = width // HEAD_DIM
    half = kv_ref.shape[1] // 2
    group = heads // (half // HEAD_DIM)
    factor = LOG2E / math.sqrt(HEAD_DIM)
    levels = []
    for r in range(sources):
        e = parts_ref[r, :, width:].astype(F32)
        levels.append(
            e + (pltpu.roll(e, HEAD_DIM - heads, 1) + pltpu.roll(e, HEAD_DIM - 2 * heads, 1))
        )
    context = []
    for h in range(heads):
        at = slice(h * HEAD_DIM, (h + 1) * HEAD_DIM)
        low = (h // group) * HEAD_DIM
        key = kv_ref[:, low : low + HEAD_DIM].astype(BF16).astype(F32)
        value = kv_ref[:, half + low : half + low + HEAD_DIM].astype(BF16).astype(F32)
        own = jnp.sum(msg_ref[:, at].astype(F32) * key, axis=1, keepdims=True) * factor
        cols = [level[:, h : h + 1] for level in levels]
        peak = own
        for c in cols:
            peak = jnp.maximum(peak, c)
        weight = jnp.exp2(own - peak)
        denom = weight
        numer = weight * value
        for r in range(sources):
            weight = jnp.exp2(cols[r] - peak)
            denom = denom + weight
            numer = numer + weight * parts_ref[r, :, at].astype(F32)
        context.append((numer / denom).astype(BF16))
    out_ref[...] = mm(jnp.concatenate(context, axis=1), w_ref[...]).astype(BF16)


def feed_kernel(tokens_ref, here_ref, there_ref, gain_ref, wg_ref, wu_ref, wd_ref, part_ref, mid_ref):
    mid = tokens_ref[...].astype(F32) + (here_ref[...].astype(F32) + there_ref[...].astype(F32))
    mid_ref[...] = mid
    normed = norm_rows(mid, gain_ref)
    gate = mm(normed, wg_ref[...])
    upper = mm(normed, wu_ref[...])
    act = (gate / (1.0 + jnp.exp(-gate)) * upper).astype(BF16)
    part_ref[...] = mm(act, wd_ref[...]).astype(BF16)


def swap(x, axis, distance):
    return lax.ppermute(x, axis, [(i, i ^ distance) for i in range(lax.axis_size(axis))])


def pair_sum(x):
    size = lax.axis_size("tp")
    distance = 1
    while distance * 2 < size:
        x = (x.astype(F32) + swap(x, "tp", distance).astype(F32)).astype(BF16)
        distance *= 2
    return x, swap(x, "tp", distance)


def in_hbm(x):
    return pltpu.with_memory_space_constraint(x, pltpu.HBM)


def in_vmem(x):
    return pltpu.with_memory_space_constraint(x, VMEM)


def per_device(
    tokens, lengths, pool_order, positions, slot_mask, kv_cache, attn_gain,
    w_query, w_key, w_value, w_out, ffn_gain, w_gate, w_up, w_down,
):
    count, model = tokens.shape
    nreq = lax.axis_size("req")
    reqs = count * nreq
    slot_count = kv_cache.shape[0]
    width = w_query.shape[1]
    half = w_key.shape[1]
    kv_heads = half // HEAD_DIM
    wide = width + HEAD_DIM
    assert slot_count % TILE == 0 and slot_count // TILE <= HEAD_DIM

    hbm_spec = pl.BlockSpec(memory_space=pltpu.HBM)
    vmem_spec = pl.BlockSpec(memory_space=VMEM)
    pair = np.arange(HEAD_DIM) % (HEAD_DIM // 2)
    freq = jnp.asarray((ROPE_BASE ** (-(pair * 2.0) / HEAD_DIM)).astype(np.float32)).reshape(1, HEAD_DIM)
    gain_shape = (model // HEAD_DIM, HEAD_DIM)

    sizes = [((count, model), BF16), ((2 * count, HEAD_DIM), F32)]
    sizes += [((reqs, reqs), BF16)] * 3
    msg, mine, normed, turn, sort, upto, back = pl.pallas_call(
        project_kernel,
        out_shape=[jax.ShapeDtypeStruct((nreq, count, wide), BF16), VMEM((count, wide), BF16)]
        + [pltpu.HBM(*size) for size in sizes],
        in_specs=[hbm_spec] * 7,
        out_specs=[vmem_spec] * 2 + [hbm_spec] * 5,
        scratch_shapes=[
            VMEM((count, model), BF16),
            VMEM(gain_shape, BF16),
            VMEM((1, count), jnp.int32),
            VMEM((1, count), jnp.int32),
            VMEM((1, HEAD_DIM), F32),
            VMEM((1, reqs), jnp.int32),
            VMEM((model, width), BF16),
        ]
        + [VMEM(*size) for size in sizes]
        + [pltpu.SemaphoreType.DMA((6 + PIECES,)), pltpu.SemaphoreType.DMA((5,))],
        compiler_params=pltpu.CompilerParams(vmem_limit_bytes=(4 + (reqs // 128) ** 2) << 20),
        cost_estimate=pl.CostEstimate(flops=2 * count * model * width, bytes_accessed=3 * model * width, transcendentals=0),
        name="project",
    )(
        in_hbm(tokens),
        in_hbm(attn_gain.reshape(gain_shape)),
        in_hbm(positions.reshape(1, count)),
        in_hbm(lengths.reshape(1, count)),
        in_hbm(freq),
        in_hbm(pool_order.reshape(1, reqs)),
        in_hbm(w_query),
    )

    everyone = lax.all_to_all(msg, "req", 0, 0).reshape(reqs, wide)

    cache = kv_cache.reshape(slot_count, 2, kv_heads, HEAD_DIM).transpose(0, 2, 1, 3)
    cache = cache.reshape(slot_count * 2 * kv_heads, HEAD_DIM)
    new_kv, keys, near, far = pl.pallas_call(
        prepare_kernel,
        out_shape=(
            VMEM((count, 2 * half), F32),
            VMEM((slot_count, half), BF16),
            VMEM((slot_count // 2, half), BF16),
            pltpu.HBM((slot_count // 2, half), BF16),
        ),
        in_specs=[hbm_spec] * 5,
        out_specs=[vmem_spec, vmem_spec, vmem_spec, hbm_spec],
        scratch_shapes=[
            VMEM((count, model), BF16),
            VMEM((2 * count, HEAD_DIM), F32),
            VMEM((model, half), BF16),
            VMEM((model, half), BF16),
            VMEM(cache.shape, BF16),
            VMEM((2, SLAB, HEAD_DIM), F32),
            VMEM((slot_count // 2, half), BF16),
            pltpu.SemaphoreType.DMA((cache.shape[0] // SLAB + 4,)),
            pltpu.SemaphoreType.DMA((cache.shape[0] // SLAB // 8,)),
        ],
        compiler_params=pltpu.CompilerParams(vmem_limit_bytes=12 << 20),
        cost_estimate=pl.CostEstimate(flops=4 * count * model * half, bytes_accessed=3 * cache.size, transcendentals=0),
        name="prepare",
    )(in_hbm(normed), in_hbm(turn), in_hbm(w_key), in_hbm(w_value), in_hbm(cache))

    live = slot_mask.reshape(slot_count // SUB, SUB)
    base = (lax.axis_index("req") * slot_count).astype(jnp.int32).reshape(1)
    rows = reqs + WIN
    heads = width // HEAD_DIM
    tiles = slot_count // TILE
    per_head = (heads, rows, HEAD_DIM)
    parts = pl.pallas_call(
        attend_kernel,
        out_shape=jax.ShapeDtypeStruct((reqs, wide), BF16),
        in_specs=[pl.BlockSpec(memory_space=pltpu.SMEM)] + [vmem_spec] * 7 + [hbm_spec] * 2,
        out_specs=vmem_spec,
        scratch_shapes=[
            VMEM(per_head, F32),
            VMEM((rows, HEAD_DIM), F32),
            VMEM((rows, HEAD_DIM), F32),
            VMEM(per_head, F32),
            VMEM(per_head, F32),
            VMEM(per_head, F32),
            VMEM((tiles, heads * WIN, TILE), F32),
            VMEM((tiles, heads * WIN, TILE), BF16),
            VMEM((slot_count, half), BF16),
            VMEM((8, HEAD_DIM), jnp.int32),
            pltpu.SMEM((8, HEAD_DIM), jnp.int32),
            pltpu.SemaphoreType.DMA,
            pltpu.SemaphoreType.DMA((2,)),
        ],
        compiler_params=pltpu.CompilerParams(vmem_limit_bytes=(4 + reqs // 32) << 20),
        cost_estimate=pl.CostEstimate(flops=1 << 30, bytes_accessed=8 << 20, transcendentals=0),
        name="attend",
    )(base, everyone, sort, upto, back, live, keys, near, in_hbm(far), in_hbm(w_gate))

    found = lax.all_to_all(parts.reshape(nreq, count, wide), "req", 0, 0)

    partial_attn = pl.pallas_call(
        output_kernel,
        out_shape=jax.ShapeDtypeStruct((count, model), BF16),
        in_specs=[vmem_spec] * 4 + [hbm_spec] * 3,
        out_specs=vmem_spec,
        compiler_params=pltpu.CompilerParams(vmem_limit_bytes=4 << 20),
        name="output",
    )(found, mine, new_kv, w_out, in_hbm(w_gate), in_hbm(w_up), in_hbm(w_down))

    here, there = pair_sum(partial_attn)
    down_part, mid = pl.pallas_call(
        feed_kernel,
        out_shape=(
            jax.ShapeDtypeStruct((count, model), BF16),
            jax.ShapeDtypeStruct((count, model), F32),
        ),
        compiler_params=pltpu.CompilerParams(vmem_limit_bytes=6 << 20),
        name="feed",
    )(tokens, here, there, ffn_gain.reshape(gain_shape), w_gate, w_up, w_down)

    here, there = pair_sum(down_part)
    hidden_out = mid + (here.astype(F32) + there.astype(F32))
    return (hidden_out, new_kv.reshape(count, 2, half))


def solution(mesh):
    placed = (
        P("req", None),
        P("req"),
        P(),
        P("req"),
        P("req"),
        P("req", None, "tp"),
        P(),
        P(None, "tp"),
        P(None, "tp"),
        P(None, "tp"),
        P("tp", None),
        P(),
        P(None, "tp"),
        P(None, "tp"),
        P("tp", None),
    )
    return jax.shard_map(
        per_device,
        mesh=mesh,
        in_specs=placed,
        out_specs=(P("req", None), P("req", None, "tp")),
        check_vma=False,
    )
```

```python
import math

import jax
import jax.numpy as jnp
import numpy as np
from jax import lax
from jax.experimental import pallas as pl
from jax.experimental.pallas import tpu as pltpu
from jax.sharding import PartitionSpec as P

HEAD_DIM = 128
ROPE_BASE = 1000000.0
EPS = 1e-05
FLOOR = -1e30
LOWEST = -1e29
LOG2E = 1.4426950408889634
TILE = 256
SUB = 128
WIN = 8
PIECES = 4
SLAB = 1024
F32 = jnp.float32
BF16 = jnp.bfloat16
VMEM = pltpu.VMEM


def mm(a, b, dims=((1,), (0,))):
    return lax.dot_general(a, b, (dims, ((), ())), preferred_element_type=F32)


def norm_rows(rows, gain_ref):
    mean_sq = jnp.mean(rows * rows, axis=-1, keepdims=True)
    scaled = rows * lax.rsqrt(mean_sq + EPS)
    gain = gain_ref[...].astype(F32)
    blocks = [
        scaled[:, i * HEAD_DIM : (i + 1) * HEAD_DIM] * gain[i : i + 1, :] for i in range(gain.shape[0])
    ]
    return jnp.concatenate(blocks, axis=1).astype(BF16)


def column(row_ref, count):
    shape = (count, count)
    diagonal = lax.broadcasted_iota(jnp.int32, shape, 0) == lax.broadcasted_iota(jnp.int32, shape, 1)
    values = jnp.broadcast_to(row_ref[...].astype(F32), shape)
    return jnp.sum(jnp.where(diagonal, values, 0.0), axis=1, keepdims=True)


def fetch(pairs, sems):
    copies = [pltpu.make_async_copy(src, dst, sems.at[i]) for i, (src, dst) in enumerate(pairs)]
    for copy in copies:
        copy.start()
    return copies


def project_kernel(
    tokens_hbm, gain_hbm, place_hbm, len_hbm, freq_hbm, order_hbm, wq_hbm,
    msg_ref, mine_ref, normed_hbm, turn_hbm, sort_hbm, upto_hbm, back_hbm,
    tokens, gain, place, lens, freq, order, wq, normed_ref, turn, sort_ref, upto_ref, back_ref, sems, out_sems,
):
    sources, count, wide = msg_ref.shape
    width = wide - HEAD_DIM
    rows = wq.shape[0] // PIECES
    small = [(tokens_hbm, tokens), (gain_hbm, gain), (place_hbm, place), (len_hbm, lens)]
    small += [(freq_hbm, freq), (order_hbm, order)]
    slabs = [pl.ds(i * rows, rows) for i in range(PIECES)]
    copies = fetch(small + [(wq_hbm.at[at, :], wq.at[at, :]) for at in slabs], sems)
    for copy in copies[: len(small)]:
        copy.wait()
    normed = norm_rows(tokens[...].astype(F32), gain)
    normed_ref[...] = normed
    lane = lax.broadcasted_iota(jnp.int32, (count, HEAD_DIM), 1)
    angle = column(place, count) * freq[...]
    cosine = jnp.cos(angle)
    sine = jnp.where(lane < HEAD_DIM // 2, -1.0, 1.0) * jnp.sin(angle)
    turn[0:count, :] = cosine
    turn[count:, :] = sine
    length = column(lens, count)
    high = jnp.floor(length * (1.0 / 128.0))
    coded = jnp.where(lane < HEAD_DIM // 2, high, length - 128.0 * high).astype(BF16)
    reqs = order.shape[1]
    row = lax.broadcasted_iota(jnp.int32, (reqs, reqs), 0)
    col = lax.broadcasted_iota(jnp.int32, (reqs, reqs), 1)
    sort = (column(order, reqs) == col.astype(F32)).astype(F32)
    sort_ref[...] = sort.astype(BF16)
    rank = jnp.sum(sort * row.astype(F32), axis=0, keepdims=True)
    upto_ref[...] = (rank <= row.astype(F32)).astype(F32).astype(BF16)
    back_ref[...] = (order[...] == row).astype(F32).astype(BF16)
    early = [(normed_ref, normed_hbm), (turn, turn_hbm), (sort_ref, sort_hbm), (upto_ref, upto_hbm), (back_ref, back_hbm)]
    outs = fetch(early, out_sems)
    q = jnp.zeros((count, width), F32)
    for copy, at in zip(copies[len(small) :], slabs):
        copy.wait()
        q = q + mm(normed[:, at.start : at.start + rows], wq[at, :])
    parts = []
    for low in range(0, width, HEAD_DIM):
        x = q[:, low : low + HEAD_DIM]
        parts.append((x * cosine + pltpu.roll(x, HEAD_DIM // 2, 1) * sine).astype(BF16))
    msg = jnp.concatenate(parts + [coded], axis=1)
    mine_ref[...] = msg
    for r in range(sources):
        msg_ref[r, :, :] = msg
    for out in outs:
        out.wait()


def prepare_kernel(
    normed_hbm, turn_hbm, wk_hbm, wv_hbm, cache_hbm,
    kv_ref, key_ref, near_ref, far_hbm,
    normed_ref, turn, wk, wv, cache, wide, far, sems, out_sems,
):
    half = wk.shape[1]
    slabs = cache.shape[0] // SLAB
    per_slot = 2 * half // HEAD_DIM
    spots = [pl.ds(i * SLAB, SLAB) for i in range(slabs)]
    wanted = [(cache_hbm.at[at, :], cache.at[at, :]) for at in spots]
    copies = fetch([(normed_hbm, normed_ref), (turn_hbm, turn), (wk_hbm, wk), (wv_hbm, wv)] + wanted, sems)
    for _ in range(3):
        copies.pop(0).wait()
    normed = normed_ref[...]
    cosine = turn[0 : turn.shape[0] // 2, :]
    sine = turn[turn.shape[0] // 2 :, :]
    k = mm(normed, wk[...])
    for low in range(0, half, HEAD_DIM):
        x = k[:, low : low + HEAD_DIM]
        kv_ref[:, low : low + HEAD_DIM] = x * cosine + pltpu.roll(x, HEAD_DIM // 2, 1) * sine
    copies.pop(0).wait()
    kv_ref[:, half:] = mm(normed, wv[...])
    slots = SLAB // per_slot
    outs = []
    for i, at in enumerate(spots):
        copies[i].wait()
        wide[i % 2, :, :] = cache[at, :].astype(F32)
        for j in range(per_slot):
            rows = wide[i % 2, pl.ds(j, slots, stride=per_slot), :].astype(BF16)
            to, first = key_ref, i * slots
            if j % 2:
                to, first = (far, first) if i < slabs // 2 else (near_ref, first - far.shape[0])
            to[first : first + slots, (j // 2) * HEAD_DIM : (j // 2 + 1) * HEAD_DIM] = rows
        if i < slabs // 2 and i % 4 == 3:
            block = pl.ds((i - 3) * slots, 4 * slots)
            outs.append(pltpu.make_async_copy(far.at[block, :], far_hbm.at[block, :], out_sems.at[i // 4]))
            outs[-1].start()
    for out in outs:
        out.wait()


def attend_kernel(
    base_ref, msg_ref, sort_ref, upto_ref, back_ref, live_ref, key_ref, near_ref, far_hbm, later_hbm,
    out_ref,
    queries, starts, ends, top, total, summed, held, weights, value_ref, ranks, ranks_s, sem, load_sems,
):
    middle = far_hbm.shape[0]
    loads = fetch(
        [
            (far_hbm, value_ref.at[pl.ds(0, middle), :]),
            (near_ref, value_ref.at[pl.ds(middle, middle), :]),
        ],
        load_sems,
    )
    reqs = msg_ref.shape[0]
    width = msg_ref.shape[1] - HEAD_DIM
    heads = width // HEAD_DIM
    group = heads // (key_ref.shape[1] // HEAD_DIM)
    tiles = key_ref.shape[0] // TILE
    factor = LOG2E / math.sqrt(HEAD_DIM)
    base = base_ref[0].astype(F32)

    lane = lax.broadcasted_iota(jnp.int32, (reqs, HEAD_DIM), 1)
    high_half = lane < HEAD_DIM // 2

    def joined(counts):
        turned = pltpu.roll(counts, HEAD_DIM // 2, 1)
        return jnp.where(high_half, 128.0 * counts + turned, counts + 128.0 * turned)

    upto = joined(mm(upto_ref[...], msg_ref[:, width:])) - base
    edge = (lane * TILE).astype(F32)
    first = jnp.sum((upto <= edge).astype(F32), axis=0, keepdims=True).astype(jnp.int32)
    begins = [first[0, t] for t in range(tiles + 1)]
    widest = begins[1] - begins[0]
    for t in range(1, tiles):
        widest = jnp.maximum(widest, begins[t + 1] - begins[t])
    ranks[0:1, :] = first
    sorted_q = mm(sort_ref[...], msg_ref[:, :width])
    far = jnp.full((WIN, HEAD_DIM), 1e9, F32)
    ends[0:reqs, :] = upto
    ends[reqs:, :] = far
    row = lax.broadcasted_iota(jnp.int32, (reqs, HEAD_DIM), 0)
    starts[0:reqs, :] = jnp.where(row == 0, -base, pltpu.roll(upto, 1, 0))
    starts[reqs:, :] = far
    for h in range(heads):
        queries[h, 0:reqs, :] = sorted_q[:, h * HEAD_DIM : (h + 1) * HEAD_DIM]
        queries[h, reqs:, :] = jnp.zeros((WIN, HEAD_DIM), F32)
    top[...] = jnp.full(top.shape, LOWEST, F32)
    total[...] = jnp.zeros(total.shape, F32)
    summed[...] = jnp.zeros(summed.shape, F32)

    def spot(h, rank):
        return (h, pl.ds(rank, WIN), slice(None))

    def of_head(x, h):
        return x[h * WIN : (h + 1) * WIN, :]

    def masked_scores(tile, rank):
        none = jnp.zeros((WIN, HEAD_DIM), BF16)
        lines = []
        for h in range(heads):
            q = queries[spot(h, rank)].astype(BF16)
            lines.append(
                jnp.concatenate([q if c == h // group else none for c in range(heads // group)], axis=1)
            )
        keys = key_ref[pl.ds(tile * TILE, TILE), :]
        scores = mm(jnp.concatenate(lines, axis=0), keys, ((1,), (1,))) * factor
        low = starts[pl.ds(rank, WIN), :]
        high = ends[pl.ds(rank, WIN), :]
        masks = []
        for i in range(TILE // SUB):
            block = tile * (TILE // SUB) + i
            at = (lax.broadcasted_iota(jnp.int32, (1, SUB), 1) + block * SUB).astype(F32)
            at = jnp.where(live_ref[pl.ds(block, 1), :] == 1, at, -1e9)
            masks.append((at >= low) & (at < high))
        mask = jnp.concatenate(masks, axis=1)
        return jnp.concatenate([jnp.where(mask, of_head(scores, h), FLOOR) for h in range(heads)], axis=0)

    def values_of(tile, weight):
        value = mm(weight, value_ref[pl.ds(tile * TILE, TILE), :])
        return [
            of_head(value, h)[:, (h // group) * HEAD_DIM : (h // group + 1) * HEAD_DIM] for h in range(heads)
        ]

    for t in range(tiles):
        held[t, :, :] = masked_scores(t, begins[t])
    peaks = [jnp.max(held[t, :, :], axis=1, keepdims=True) for t in range(tiles)]
    for t in range(tiles):
        for h in range(heads):
            at = spot(h, begins[t])
            top[at] = jnp.maximum(top[at], of_head(peaks[t], h))
    counts = []
    for t in range(tiles):
        peak = jnp.concatenate([top[spot(h, begins[t])] for h in range(heads)], axis=0)
        weight = jnp.exp2(held[t, :, :] - jnp.concatenate([peak] * (TILE // HEAD_DIM), axis=1))
        weights[t, :, :] = weight.astype(BF16)
        counts.append(jnp.sum(weight, axis=1, keepdims=True))
    loads[0].wait()
    loads[1].wait()
    found = [values_of(t, weights[t, :, :]) for t in range(tiles)]
    for t in range(tiles):
        for h in range(heads):
            at = spot(h, begins[t])
            total[at] = total[at] + of_head(counts[t], h)
            summed[at] = summed[at] + found[t][h]

    def more(t, carry):
        begin = ranks_s[0, t]

        def again(i, inner):
            rank = begin + (i + 1) * WIN
            masked = masked_scores(t, rank)
            peak = jnp.maximum(jnp.max(masked, axis=1, keepdims=True), LOWEST)
            weight = jnp.exp2(masked - peak)
            count = jnp.sum(weight, axis=1, keepdims=True)
            value = values_of(t, weight.astype(BF16))
            for h in range(heads):
                at = spot(h, rank)
                old = top[at]
                new = jnp.maximum(old, of_head(peak, h))
                left = jnp.exp2(old - new)
                right = jnp.exp2(of_head(peak, h) - new)
                top[at] = new
                total[at] = total[at] * left + of_head(count, h) * right
                summed[at] = summed[at] * left + value[h] * right
            return inner

        return lax.fori_loop(0, (ranks_s[0, t + 1] - begin) // WIN, again, carry)

    @pl.when(widest >= WIN)
    def _():
        copy = pltpu.make_async_copy(ranks, ranks_s, sem)
        copy.start()
        copy.wait()
        lax.fori_loop(0, tiles, more, 0)

    columns = []
    sums = jnp.ones((reqs, HEAD_DIM), F32)
    peaks = jnp.zeros((reqs, HEAD_DIM), F32)
    for h in range(heads):
        count = total[h, 0:reqs, :]
        columns.append((summed[h, 0:reqs, :] / jnp.where(count > 0.0, count, 1.0)).astype(BF16))
        sums = jnp.where(lane % heads == h, count, sums)
        peaks = jnp.where(lane % heads == h, top[h, 0:reqs, :], peaks)
    some = sums > 0.0
    rest = jnp.where(some, peaks + jnp.log2(jnp.where(some, sums, 1.0)), LOWEST)
    extra = jnp.zeros((reqs, HEAD_DIM), F32)
    for piece in range(3):
        coded = rest.astype(BF16).astype(F32)
        extra = jnp.where(lane // heads == piece, coded, extra)
        rest = rest - coded
    both = jnp.concatenate(columns + [extra.astype(BF16)], axis=1)
    out_ref[...] = mm(back_ref[...], both).astype(BF16)


def output_kernel(parts_ref, msg_ref, kv_ref, w_ref, *rest):
    out_ref = rest[-1]
    sources, count, wide = parts_ref.shape
    width = wide - HEAD_DIM
    heads = width // HEAD_DIM
    half = kv_ref.shape[1] // 2
    group = heads // (half // HEAD_DIM)
    factor = LOG2E / math.sqrt(HEAD_DIM)
    levels = []
    for r in range(sources):
        e = parts_ref[r, :, width:].astype(F32)
        levels.append(
            e + (pltpu.roll(e, HEAD_DIM - heads, 1) + pltpu.roll(e, HEAD_DIM - 2 * heads, 1))
        )
    context = []
    for h in range(heads):
        at = slice(h * HEAD_DIM, (h + 1) * HEAD_DIM)
        low = (h // group) * HEAD_DIM
        key = kv_ref[:, low : low + HEAD_DIM].astype(BF16).astype(F32)
        value = kv_ref[:, half + low : half + low + HEAD_DIM].astype(BF16).astype(F32)
        own = jnp.sum(msg_ref[:, at].astype(F32) * key, axis=1, keepdims=True) * factor
        cols = [level[:, h : h + 1] for level in levels]
        peak = own
        for c in cols:
            peak = jnp.maximum(peak, c)
        weight = jnp.exp2(own - peak)
        denom = weight
        numer = weight * value
        for r in range(sources):
            weight = jnp.exp2(cols[r] - peak)
            denom = denom + weight
            numer = numer + weight * parts_ref[r, :, at].astype(F32)
        context.append((numer / denom).astype(BF16))
    out_ref[...] = mm(jnp.concatenate(context, axis=1), w_ref[...]).astype(BF16)


def feed_kernel(tokens_ref, here_ref, there_ref, gain_ref, wg_ref, wu_ref, wd_ref, part_ref, mid_ref):
    mid = tokens_ref[...].astype(F32) + (here_ref[...].astype(F32) + there_ref[...].astype(F32))
    mid_ref[...] = mid
    normed = norm_rows(mid, gain_ref)
    gate = mm(normed, wg_ref[...])
    upper = mm(normed, wu_ref[...])
    act = (gate / (1.0 + jnp.exp(-gate)) * upper).astype(BF16)
    part_ref[...] = mm(act, wd_ref[...]).astype(BF16)


def swap(x, axis, distance):
    return lax.ppermute(x, axis, [(i, i ^ distance) for i in range(lax.axis_size(axis))])


def pair_sum(x):
    size = lax.axis_size("tp")
    distance = 1
    while distance * 2 < size:
        x = (x.astype(F32) + swap(x, "tp", distance).astype(F32)).astype(BF16)
        distance *= 2
    return x, swap(x, "tp", distance)


def in_hbm(x):
    return pltpu.with_memory_space_constraint(x, pltpu.HBM)


def in_vmem(x):
    return pltpu.with_memory_space_constraint(x, VMEM)


def per_device(
    tokens, lengths, pool_order, positions, slot_mask, kv_cache, attn_gain,
    w_query, w_key, w_value, w_out, ffn_gain, w_gate, w_up, w_down,
):
    count, model = tokens.shape
    nreq = lax.axis_size("req")
    reqs = count * nreq
    slot_count = kv_cache.shape[0]
    width = w_query.shape[1]
    half = w_key.shape[1]
    kv_heads = half // HEAD_DIM
    wide = width + HEAD_DIM
    assert slot_count % TILE == 0 and slot_count // TILE < HEAD_DIM

    hbm_spec = pl.BlockSpec(memory_space=pltpu.HBM)
    vmem_spec = pl.BlockSpec(memory_space=VMEM)
    pair = np.arange(HEAD_DIM) % (HEAD_DIM // 2)
    freq = jnp.asarray((ROPE_BASE ** (-(pair * 2.0) / HEAD_DIM)).astype(np.float32)).reshape(1, HEAD_DIM)
    gain_shape = (model // HEAD_DIM, HEAD_DIM)

    sizes = [((count, model), BF16), ((2 * count, HEAD_DIM), F32)]
    sizes += [((reqs, reqs), BF16)] * 3
    msg, mine, normed, turn, sort, upto, back = pl.pallas_call(
        project_kernel,
        out_shape=[jax.ShapeDtypeStruct((nreq, count, wide), BF16), VMEM((count, wide), BF16)]
        + [pltpu.HBM(*size) for size in sizes],
        in_specs=[hbm_spec] * 7,
        out_specs=[vmem_spec] * 2 + [hbm_spec] * 5,
        scratch_shapes=[
            VMEM((count, model), BF16),
            VMEM(gain_shape, BF16),
            VMEM((1, count), jnp.int32),
            VMEM((1, count), jnp.int32),
            VMEM((1, HEAD_DIM), F32),
            VMEM((1, reqs), jnp.int32),
            VMEM((model, width), BF16),
        ]
        + [VMEM(*size) for size in sizes]
        + [pltpu.SemaphoreType.DMA((6 + PIECES,)), pltpu.SemaphoreType.DMA((5,))],
        compiler_params=pltpu.CompilerParams(vmem_limit_bytes=(4 + (reqs // 128) ** 2) << 20),
        cost_estimate=pl.CostEstimate(flops=2 * count * model * width, bytes_accessed=3 * model * width, transcendentals=0),
        name="project",
    )(
        in_hbm(tokens),
        in_hbm(attn_gain.reshape(gain_shape)),
        in_hbm(positions.reshape(1, count)),
        in_hbm(lengths.reshape(1, count)),
        in_hbm(freq),
        in_hbm(pool_order.reshape(1, reqs)),
        in_hbm(w_query),
    )

    everyone = lax.all_to_all(msg, "req", 0, 0).reshape(reqs, wide)

    cache = kv_cache.reshape(slot_count, 2, kv_heads, HEAD_DIM).transpose(0, 2, 1, 3)
    cache = cache.reshape(slot_count * 2 * kv_heads, HEAD_DIM)
    new_kv, keys, near, far = pl.pallas_call(
        prepare_kernel,
        out_shape=(
            VMEM((count, 2 * half), F32),
            VMEM((slot_count, half), BF16),
            VMEM((slot_count // 2, half), BF16),
            pltpu.HBM((slot_count // 2, half), BF16),
        ),
        in_specs=[hbm_spec] * 5,
        out_specs=[vmem_spec, vmem_spec, vmem_spec, hbm_spec],
        scratch_shapes=[
            VMEM((count, model), BF16),
            VMEM((2 * count, HEAD_DIM), F32),
            VMEM((model, half), BF16),
            VMEM((model, half), BF16),
            VMEM(cache.shape, BF16),
            VMEM((2, SLAB, HEAD_DIM), F32),
            VMEM((slot_count // 2, half), BF16),
            pltpu.SemaphoreType.DMA((cache.shape[0] // SLAB + 4,)),
            pltpu.SemaphoreType.DMA((cache.shape[0] // SLAB // 8,)),
        ],
        compiler_params=pltpu.CompilerParams(vmem_limit_bytes=12 << 20),
        cost_estimate=pl.CostEstimate(flops=4 * count * model * half, bytes_accessed=3 * cache.size, transcendentals=0),
        name="prepare",
    )(in_hbm(normed), in_hbm(turn), in_hbm(w_key), in_hbm(w_value), in_hbm(cache))

    live = slot_mask.reshape(slot_count // SUB, SUB)
    base = (lax.axis_index("req") * slot_count).astype(jnp.int32).reshape(1)
    rows = reqs + WIN
    heads = width // HEAD_DIM
    tiles = slot_count // TILE
    per_head = (heads, rows, HEAD_DIM)
    parts = pl.pallas_call(
        attend_kernel,
        out_shape=jax.ShapeDtypeStruct((reqs, wide), BF16),
        in_specs=[pl.BlockSpec(memory_space=pltpu.SMEM)] + [vmem_spec] * 7 + [hbm_spec] * 2,
        out_specs=vmem_spec,
        scratch_shapes=[
            VMEM(per_head, F32),
            VMEM((rows, HEAD_DIM), F32),
            VMEM((rows, HEAD_DIM), F32),
            VMEM(per_head, F32),
            VMEM(per_head, F32),
            VMEM(per_head, F32),
            VMEM((tiles, heads * WIN, TILE), F32),
            VMEM((tiles, heads * WIN, TILE), BF16),
            VMEM((slot_count, half), BF16),
            VMEM((8, HEAD_DIM), jnp.int32),
            pltpu.SMEM((8, HEAD_DIM), jnp.int32),
            pltpu.SemaphoreType.DMA,
            pltpu.SemaphoreType.DMA((2,)),
        ],
        compiler_params=pltpu.CompilerParams(vmem_limit_bytes=(4 + reqs // 32) << 20),
        cost_estimate=pl.CostEstimate(flops=1 << 30, bytes_accessed=8 << 20, transcendentals=0),
        name="attend",
    )(base, everyone, sort, upto, back, live, keys, near, in_hbm(far), in_hbm(w_gate))

    found = lax.all_to_all(parts.reshape(nreq, count, wide), "req", 0, 0)

    partial_attn = pl.pallas_call(
        output_kernel,
        out_shape=jax.ShapeDtypeStruct((count, model), BF16),
        in_specs=[vmem_spec] * 4 + [hbm_spec] * 3,
        out_specs=vmem_spec,
        compiler_params=pltpu.CompilerParams(vmem_limit_bytes=4 << 20),
        name="output",
    )(found, mine, new_kv, w_out, in_hbm(w_gate), in_hbm(w_up), in_hbm(w_down))

    here, there = pair_sum(partial_attn)
    down_part, mid = pl.pallas_call(
        feed_kernel,
        out_shape=(
            jax.ShapeDtypeStruct((count, model), BF16),
            jax.ShapeDtypeStruct((count, model), F32),
        ),
        compiler_params=pltpu.CompilerParams(vmem_limit_bytes=6 << 20),
        name="feed",
    )(tokens, here, there, ffn_gain.reshape(gain_shape), w_gate, w_up, w_down)

    here, there = pair_sum(down_part)
    hidden_out = mid + (here.astype(F32) + there.astype(F32))
    return (hidden_out, new_kv.reshape(count, 2, half))


def solution(mesh):
    placed = (
        P("req", None),
        P("req"),
        P(),
        P("req"),
        P("req"),
        P("req", None, "tp"),
        P(),
        P(None, "tp"),
        P(None, "tp"),
        P(None, "tp"),
        P("tp", None),
        P(),
        P(None, "tp"),
        P(None, "tp"),
        P("tp", None),
    )
    return jax.shard_map(
        per_device,
        mesh=mesh,
        in_specs=placed,
        out_specs=(P("req", None), P("req", None, "tp")),
        check_vma=False,
    )
```

```python
import math

import jax
import jax.numpy as jnp
import numpy as np
from jax import lax
from jax.experimental import pallas as pl
from jax.experimental.pallas import tpu as pltpu
from jax.sharding import PartitionSpec as P

HEAD_DIM = 128
ROPE_BASE = 1000000.0
EPS = 1e-05
FLOOR = -1e30
LOWEST = -1e29
LOG2E = 1.4426950408889634
TILE = 256
SUB = 128
WIN = 8
PIECES = 4
SLAB = 1024
F32 = jnp.float32
BF16 = jnp.bfloat16
VMEM = pltpu.VMEM


def mm(a, b, dims=((1,), (0,))):
    return lax.dot_general(a, b, (dims, ((), ())), preferred_element_type=F32)


def norm_rows(rows, gain_ref):
    mean_sq = jnp.mean(rows * rows, axis=-1, keepdims=True)
    scaled = rows * lax.rsqrt(mean_sq + EPS)
    gain = gain_ref[...].astype(F32)
    blocks = [
        scaled[:, i * HEAD_DIM : (i + 1) * HEAD_DIM] * gain[i : i + 1, :] for i in range(gain.shape[0])
    ]
    return jnp.concatenate(blocks, axis=1).astype(BF16)


def column(row_ref, count):
    shape = (count, count)
    diagonal = lax.broadcasted_iota(jnp.int32, shape, 0) == lax.broadcasted_iota(jnp.int32, shape, 1)
    values = jnp.broadcast_to(row_ref[...].astype(F32), shape)
    return jnp.sum(jnp.where(diagonal, values, 0.0), axis=1, keepdims=True)


def fetch(pairs, sems):
    copies = [pltpu.make_async_copy(src, dst, sems.at[i]) for i, (src, dst) in enumerate(pairs)]
    for copy in copies:
        copy.start()
    return copies


def project_kernel(
    tokens_hbm, gain_hbm, place_hbm, len_hbm, freq_hbm, order_hbm, wq_hbm,
    msg_ref, mine_ref, normed_hbm, turn_hbm, sort_hbm, upto_hbm, back_hbm,
    tokens, gain, place, lens, freq, order, wq, normed_ref, turn, sort_ref, upto_ref, back_ref, sems, out_sems,
):
    sources, count, wide = msg_ref.shape
    width = wide - HEAD_DIM
    rows = wq.shape[0] // PIECES
    small = [(tokens_hbm, tokens), (gain_hbm, gain), (place_hbm, place), (len_hbm, lens)]
    small += [(freq_hbm, freq), (order_hbm, order)]
    slabs = [pl.ds(i * rows, rows) for i in range(PIECES)]
    copies = fetch(small + [(wq_hbm.at[at, :], wq.at[at, :]) for at in slabs], sems)
    for copy in copies[: len(small)]:
        copy.wait()
    normed = norm_rows(tokens[...].astype(F32), gain)
    normed_ref[...] = normed
    lane = lax.broadcasted_iota(jnp.int32, (count, HEAD_DIM), 1)
    angle = column(place, count) * freq[...]
    cosine = jnp.cos(angle)
    sine = jnp.where(lane < HEAD_DIM // 2, -1.0, 1.0) * jnp.sin(angle)
    turn[0:count, :] = cosine
    turn[count:, :] = sine
    length = column(lens, count)
    high = jnp.floor(length * (1.0 / 128.0))
    coded = jnp.where(lane < HEAD_DIM // 2, high, length - 128.0 * high).astype(BF16)
    reqs = order.shape[1]
    row = lax.broadcasted_iota(jnp.int32, (reqs, reqs), 0)
    col = lax.broadcasted_iota(jnp.int32, (reqs, reqs), 1)
    sort = (column(order, reqs) == col.astype(F32)).astype(F32)
    sort_ref[...] = sort.astype(BF16)
    rank = jnp.sum(sort * row.astype(F32), axis=0, keepdims=True)
    upto_ref[...] = (rank <= row.astype(F32)).astype(F32).astype(BF16)
    back_ref[...] = (order[...] == row).astype(F32).astype(BF16)
    early = [(normed_ref, normed_hbm), (turn, turn_hbm), (sort_ref, sort_hbm), (upto_ref, upto_hbm), (back_ref, back_hbm)]
    outs = fetch(early, out_sems)
    q = jnp.zeros((count, width), F32)
    for copy, at in zip(copies[len(small) :], slabs):
        copy.wait()
        q = q + mm(normed[:, at.start : at.start + rows], wq[at, :])
    parts = []
    for low in range(0, width, HEAD_DIM):
        x = q[:, low : low + HEAD_DIM]
        parts.append((x * cosine + pltpu.roll(x, HEAD_DIM // 2, 1) * sine).astype(BF16))
    msg = jnp.concatenate(parts + [coded], axis=1)
    mine_ref[...] = msg
    for r in range(sources):
        msg_ref[r, :, :] = msg
    for out in outs:
        out.wait()


def prepare_kernel(
    normed_hbm, turn_hbm, wk_hbm, wv_hbm, cache_hbm,
    kv_ref, key_ref, near_ref, far_hbm,
    normed_ref, turn, wk, wv, cache, wide, far, sems, out_sems,
):
    half = wk.shape[1]
    slabs = cache.shape[0] // SLAB
    per_slot = 2 * half // HEAD_DIM
    spots = [pl.ds(i * SLAB, SLAB) for i in range(slabs)]
    wanted = [(cache_hbm.at[at, :], cache.at[at, :]) for at in spots]
    copies = fetch([(normed_hbm, normed_ref), (turn_hbm, turn), (wk_hbm, wk), (wv_hbm, wv)] + wanted, sems)
    for _ in range(3):
        copies.pop(0).wait()
    normed = normed_ref[...]
    cosine = turn[0 : turn.shape[0] // 2, :]
    sine = turn[turn.shape[0] // 2 :, :]
    k = mm(normed, wk[...])
    for low in range(0, half, HEAD_DIM):
        x = k[:, low : low + HEAD_DIM]
        kv_ref[:, low : low + HEAD_DIM] = x * cosine + pltpu.roll(x, HEAD_DIM // 2, 1) * sine
    copies.pop(0).wait()
    kv_ref[:, half:] = mm(normed, wv[...])
    slots = SLAB // per_slot
    outs = []
    for i, at in enumerate(spots):
        copies[i].wait()
        wide[i % 2, :, :] = cache[at, :].astype(F32)
        for j in range(per_slot):
            rows = wide[i % 2, pl.ds(j, slots, stride=per_slot), :].astype(BF16)
            to, first = key_ref, i * slots
            if j % 2:
                to, first = (far, first) if i < slabs // 2 else (near_ref, first - far.shape[0])
            to[first : first + slots, (j // 2) * HEAD_DIM : (j // 2 + 1) * HEAD_DIM] = rows
        if i < slabs // 2 and i % 4 == 3:
            block = pl.ds((i - 3) * slots, 4 * slots)
            outs.append(pltpu.make_async_copy(far.at[block, :], far_hbm.at[block, :], out_sems.at[i // 4]))
            outs[-1].start()
    for out in outs:
        out.wait()


def attend_kernel(
    base_ref, msg_ref, sort_ref, upto_ref, back_ref, live_ref, key_ref, near_ref, far_hbm, later_hbm,
    out_ref,
    queries, starts, ends, top, total, summed, held, weights, value_ref, ranks, ranks_s, sem, load_sems,
):
    middle = far_hbm.shape[0]
    loads = fetch(
        [
            (far_hbm, value_ref.at[pl.ds(0, middle), :]),
            (near_ref, value_ref.at[pl.ds(middle, middle), :]),
        ],
        load_sems,
    )
    reqs = msg_ref.shape[0]
    width = msg_ref.shape[1] - HEAD_DIM
    heads = width // HEAD_DIM
    group = heads // (key_ref.shape[1] // HEAD_DIM)
    tiles = key_ref.shape[0] // TILE
    factor = LOG2E / math.sqrt(HEAD_DIM)
    base = base_ref[0].astype(F32)

    lane = lax.broadcasted_iota(jnp.int32, (reqs, HEAD_DIM), 1)
    high_half = lane < HEAD_DIM // 2

    def joined(counts):
        turned = pltpu.roll(counts, HEAD_DIM // 2, 1)
        return jnp.where(high_half, 128.0 * counts + turned, counts + 128.0 * turned)

    upto = joined(mm(upto_ref[...], msg_ref[:, width:])) - base
    edge = (lane * TILE).astype(F32)
    first = jnp.sum((upto <= edge).astype(F32), axis=0, keepdims=True).astype(jnp.int32)
    begins = [first[0, t] for t in range(tiles + 1)]
    widest = begins[1] - begins[0]
    for t in range(1, tiles):
        widest = jnp.maximum(widest, begins[t + 1] - begins[t])
    ranks[0:1, :] = first
    sorted_q = mm(sort_ref[...], msg_ref[:, :width])
    far = jnp.full((WIN, HEAD_DIM), 1e9, F32)
    ends[0:reqs, :] = upto
    ends[reqs:, :] = far
    row = lax.broadcasted_iota(jnp.int32, (reqs, HEAD_DIM), 0)
    starts[0:reqs, :] = jnp.where(row == 0, -base, pltpu.roll(upto, 1, 0))
    starts[reqs:, :] = far
    for h in range(heads):
        queries[h, 0:reqs, :] = sorted_q[:, h * HEAD_DIM : (h + 1) * HEAD_DIM]
        queries[h, reqs:, :] = jnp.zeros((WIN, HEAD_DIM), F32)
    top[...] = jnp.full(top.shape, LOWEST, F32)
    total[...] = jnp.zeros(total.shape, F32)
    summed[...] = jnp.zeros(summed.shape, F32)

    def spot(h, rank):
        return (h, pl.ds(rank, WIN), slice(None))

    def of_head(x, h):
        return x[h * WIN : (h + 1) * WIN, :]

    def masked_scores(tile, rank):
        none = jnp.zeros((WIN, HEAD_DIM), BF16)
        lines = []
        for h in range(heads):
            q = queries[spot(h, rank)].astype(BF16)
            lines.append(
                jnp.concatenate([q if c == h // group else none for c in range(heads // group)], axis=1)
            )
        keys = key_ref[pl.ds(tile * TILE, TILE), :]
        scores = mm(jnp.concatenate(lines, axis=0), keys, ((1,), (1,))) * factor
        low = starts[pl.ds(rank, WIN), :]
        high = ends[pl.ds(rank, WIN), :]
        masks = []
        for i in range(TILE // SUB):
            block = tile * (TILE // SUB) + i
            at = (lax.broadcasted_iota(jnp.int32, (1, SUB), 1) + block * SUB).astype(F32)
            at = jnp.where(live_ref[pl.ds(block, 1), :] == 1, at, -1e9)
            masks.append((at >= low) & (at < high))
        mask = jnp.concatenate(masks, axis=1)
        return jnp.concatenate([jnp.where(mask, of_head(scores, h), FLOOR) for h in range(heads)], axis=0)

    def values_of(tile, weight):
        value = mm(weight, value_ref[pl.ds(tile * TILE, TILE), :])
        return [
            of_head(value, h)[:, (h // group) * HEAD_DIM : (h // group + 1) * HEAD_DIM] for h in range(heads)
        ]

    for t in range(tiles):
        held[t, :, :] = masked_scores(t, begins[t])
    peaks = [jnp.max(held[t, :, :], axis=1, keepdims=True) for t in range(tiles)]
    for t in range(tiles):
        for h in range(heads):
            at = spot(h, begins[t])
            top[at] = jnp.maximum(top[at], of_head(peaks[t], h))
    counts = []
    for t in range(tiles):
        peak = jnp.concatenate([top[spot(h, begins[t])] for h in range(heads)], axis=0)
        weight = jnp.exp2(held[t, :, :] - jnp.concatenate([peak] * (TILE // HEAD_DIM), axis=1))
        weights[t, :, :] = weight.astype(BF16)
        counts.append(jnp.sum(weight, axis=1, keepdims=True))
    loads[0].wait()
    loads[1].wait()
    found = [values_of(t, weights[t, :, :]) for t in range(tiles)]
    for t in range(tiles):
        for h in range(heads):
            at = spot(h, begins[t])
            total[at] = total[at] + of_head(counts[t], h)
            summed[at] = summed[at] + found[t][h]

    def more(t, carry):
        begin = ranks_s[0, t]

        def again(i, inner):
            rank = begin + (i + 1) * WIN
            masked = masked_scores(t, rank)
            peak = jnp.maximum(jnp.max(masked, axis=1, keepdims=True), LOWEST)
            weight = jnp.exp2(masked - peak)
            count = jnp.sum(weight, axis=1, keepdims=True)
            value = values_of(t, weight.astype(BF16))
            for h in range(heads):
                at = spot(h, rank)
                old = top[at]
                new = jnp.maximum(old, of_head(peak, h))
                left = jnp.exp2(old - new)
                right = jnp.exp2(of_head(peak, h) - new)
                top[at] = new
                total[at] = total[at] * left + of_head(count, h) * right
                summed[at] = summed[at] * left + value[h] * right
            return inner

        return lax.fori_loop(0, (ranks_s[0, t + 1] - begin) // WIN, again, carry)

    @pl.when(widest >= WIN)
    def _():
        copy = pltpu.make_async_copy(ranks, ranks_s, sem)
        copy.start()
        copy.wait()
        lax.fori_loop(0, tiles, more, 0)

    columns = []
    sums = jnp.ones((reqs, HEAD_DIM), F32)
    peaks = jnp.zeros((reqs, HEAD_DIM), F32)
    for h in range(heads):
        count = total[h, 0:reqs, :]
        columns.append((summed[h, 0:reqs, :] / jnp.where(count > 0.0, count, 1.0)).astype(BF16))
        sums = jnp.where(lane % heads == h, count, sums)
        peaks = jnp.where(lane % heads == h, top[h, 0:reqs, :], peaks)
    some = sums > 0.0
    rest = jnp.where(some, peaks + jnp.log2(jnp.where(some, sums, 1.0)), LOWEST)
    extra = jnp.zeros((reqs, HEAD_DIM), F32)
    for piece in range(3):
        coded = rest.astype(BF16).astype(F32)
        extra = jnp.where(lane // heads == piece, coded, extra)
        rest = rest - coded
    both = jnp.concatenate(columns + [extra.astype(BF16)], axis=1)
    out_ref[...] = mm(back_ref[...], both).astype(BF16)


def output_kernel(parts_ref, msg_ref, kv_ref, w_ref, *rest):
    out_ref = rest[-1]
    sources, count, wide = parts_ref.shape
    width = wide - HEAD_DIM
    heads = width // HEAD_DIM
    half = kv_ref.shape[1] // 2
    group = heads // (half // HEAD_DIM)
    factor = LOG2E / math.sqrt(HEAD_DIM)
    levels = []
    for r in range(sources):
        e = parts_ref[r, :, width:].astype(F32)
        levels.append(
            e + (pltpu.roll(e, HEAD_DIM - heads, 1) + pltpu.roll(e, HEAD_DIM - 2 * heads, 1))
        )
    context = []
    for h in range(heads):
        at = slice(h * HEAD_DIM, (h + 1) * HEAD_DIM)
        low = (h // group) * HEAD_DIM
        key = kv_ref[:, low : low + HEAD_DIM].astype(BF16).astype(F32)
        value = kv_ref[:, half + low : half + low + HEAD_DIM].astype(BF16).astype(F32)
        own = jnp.sum(msg_ref[:, at].astype(F32) * key, axis=1, keepdims=True) * factor
        cols = [level[:, h : h + 1] for level in levels]
        peak = own
        for c in cols:
            peak = jnp.maximum(peak, c)
        weight = jnp.exp2(own - peak)
        denom = weight
        numer = weight * value
        for r in range(sources):
            weight = jnp.exp2(cols[r] - peak)
            denom = denom + weight
            numer = numer + weight * parts_ref[r, :, at].astype(F32)
        context.append((numer / denom).astype(BF16))
    out_ref[...] = mm(jnp.concatenate(context, axis=1), w_ref[...]).astype(BF16)


def feed_kernel(tokens_ref, here_ref, there_ref, gain_ref, wg_ref, wu_ref, wd_ref, part_ref, mid_ref):
    mid = tokens_ref[...].astype(F32) + (here_ref[...].astype(F32) + there_ref[...].astype(F32))
    mid_ref[...] = mid
    normed = norm_rows(mid, gain_ref)
    gate = mm(normed, wg_ref[...])
    upper = mm(normed, wu_ref[...])
    act = (gate / (1.0 + jnp.exp(-gate)) * upper).astype(BF16)
    part_ref[...] = mm(act, wd_ref[...]).astype(BF16)


def swap(x, axis, distance):
    return lax.ppermute(x, axis, [(i, i ^ distance) for i in range(lax.axis_size(axis))])


def pair_sum(x):
    size = lax.axis_size("tp")
    distance = 1
    while 2 * distance < size - 1:
        x = (x.astype(F32) + swap(x, "tp", distance).astype(F32)).astype(BF16)
        distance = 2 * distance + 1
    return x, swap(x, "tp", distance)


def in_hbm(x):
    return pltpu.with_memory_space_constraint(x, pltpu.HBM)


def in_vmem(x):
    return pltpu.with_memory_space_constraint(x, VMEM)


def per_device(
    tokens, lengths, pool_order, positions, slot_mask, kv_cache, attn_gain,
    w_query, w_key, w_value, w_out, ffn_gain, w_gate, w_up, w_down,
):
    count, model = tokens.shape
    nreq = lax.axis_size("req")
    reqs = count * nreq
    slot_count = kv_cache.shape[0]
    width = w_query.shape[1]
    half = w_key.shape[1]
    kv_heads = half // HEAD_DIM
    wide = width + HEAD_DIM
    assert slot_count % TILE == 0 and slot_count // TILE < HEAD_DIM

    hbm_spec = pl.BlockSpec(memory_space=pltpu.HBM)
    vmem_spec = pl.BlockSpec(memory_space=VMEM)
    pair = np.arange(HEAD_DIM) % (HEAD_DIM // 2)
    freq = jnp.asarray((ROPE_BASE ** (-(pair * 2.0) / HEAD_DIM)).astype(np.float32)).reshape(1, HEAD_DIM)
    gain_shape = (model // HEAD_DIM, HEAD_DIM)

    sizes = [((count, model), BF16), ((2 * count, HEAD_DIM), F32)]
    sizes += [((reqs, reqs), BF16)] * 3
    msg, mine, normed, turn, sort, upto, back = pl.pallas_call(
        project_kernel,
        out_shape=[jax.ShapeDtypeStruct((nreq, count, wide), BF16), VMEM((count, wide), BF16)]
        + [pltpu.HBM(*size) for size in sizes],
        in_specs=[hbm_spec] * 7,
        out_specs=[vmem_spec] * 2 + [hbm_spec] * 5,
        scratch_shapes=[
            VMEM((count, model), BF16),
            VMEM(gain_shape, BF16),
            VMEM((1, count), jnp.int32),
            VMEM((1, count), jnp.int32),
            VMEM((1, HEAD_DIM), F32),
            VMEM((1, reqs), jnp.int32),
            VMEM((model, width), BF16),
        ]
        + [VMEM(*size) for size in sizes]
        + [pltpu.SemaphoreType.DMA((6 + PIECES,)), pltpu.SemaphoreType.DMA((5,))],
        compiler_params=pltpu.CompilerParams(vmem_limit_bytes=(4 + (reqs // 128) ** 2) << 20),
        cost_estimate=pl.CostEstimate(flops=2 * count * model * width, bytes_accessed=3 * model * width, transcendentals=0),
        name="project",
    )(
        in_hbm(tokens),
        in_hbm(attn_gain.reshape(gain_shape)),
        in_hbm(positions.reshape(1, count)),
        in_hbm(lengths.reshape(1, count)),
        in_hbm(freq),
        in_hbm(pool_order.reshape(1, reqs)),
        in_hbm(w_query),
    )

    everyone = lax.all_to_all(msg, "req", 0, 0).reshape(reqs, wide)

    cache = kv_cache.reshape(slot_count, 2, kv_heads, HEAD_DIM).transpose(0, 2, 1, 3)
    cache = cache.reshape(slot_count * 2 * kv_heads, HEAD_DIM)
    new_kv, keys, near, far = pl.pallas_call(
        prepare_kernel,
        out_shape=(
            VMEM((count, 2 * half), F32),
            VMEM((slot_count, half), BF16),
            VMEM((slot_count // 2, half), BF16),
            pltpu.HBM((slot_count // 2, half), BF16),
        ),
        in_specs=[hbm_spec] * 5,
        out_specs=[vmem_spec, vmem_spec, vmem_spec, hbm_spec],
        scratch_shapes=[
            VMEM((count, model), BF16),
            VMEM((2 * count, HEAD_DIM), F32),
            VMEM((model, half), BF16),
            VMEM((model, half), BF16),
            VMEM(cache.shape, BF16),
            VMEM((2, SLAB, HEAD_DIM), F32),
            VMEM((slot_count // 2, half), BF16),
            pltpu.SemaphoreType.DMA((cache.shape[0] // SLAB + 4,)),
            pltpu.SemaphoreType.DMA((cache.shape[0] // SLAB // 8,)),
        ],
        compiler_params=pltpu.CompilerParams(vmem_limit_bytes=12 << 20),
        cost_estimate=pl.CostEstimate(flops=4 * count * model * half, bytes_accessed=3 * cache.size, transcendentals=0),
        name="prepare",
    )(in_hbm(normed), in_hbm(turn), in_hbm(w_key), in_hbm(w_value), in_hbm(cache))

    live = slot_mask.reshape(slot_count // SUB, SUB)
    base = (lax.axis_index("req") * slot_count).astype(jnp.int32).reshape(1)
    rows = reqs + WIN
    heads = width // HEAD_DIM
    tiles = slot_count // TILE
    per_head = (heads, rows, HEAD_DIM)
    parts = pl.pallas_call(
        attend_kernel,
        out_shape=jax.ShapeDtypeStruct((reqs, wide), BF16),
        in_specs=[pl.BlockSpec(memory_space=pltpu.SMEM)] + [vmem_spec] * 7 + [hbm_spec] * 2,
        out_specs=vmem_spec,
        scratch_shapes=[
            VMEM(per_head, F32),
            VMEM((rows, HEAD_DIM), F32),
            VMEM((rows, HEAD_DIM), F32),
            VMEM(per_head, F32),
            VMEM(per_head, F32),
            VMEM(per_head, F32),
            VMEM((tiles, heads * WIN, TILE), F32),
            VMEM((tiles, heads * WIN, TILE), BF16),
            VMEM((slot_count, half), BF16),
            VMEM((8, HEAD_DIM), jnp.int32),
            pltpu.SMEM((8, HEAD_DIM), jnp.int32),
            pltpu.SemaphoreType.DMA,
            pltpu.SemaphoreType.DMA((2,)),
        ],
        compiler_params=pltpu.CompilerParams(vmem_limit_bytes=(4 + reqs // 32) << 20),
        cost_estimate=pl.CostEstimate(flops=1 << 30, bytes_accessed=8 << 20, transcendentals=0),
        name="attend",
    )(base, everyone, sort, upto, back, live, keys, near, in_hbm(far), in_hbm(w_gate))

    found = lax.all_to_all(parts.reshape(nreq, count, wide), "req", 0, 0)

    partial_attn = pl.pallas_call(
        output_kernel,
        out_shape=jax.ShapeDtypeStruct((count, model), BF16),
        in_specs=[vmem_spec] * 4 + [hbm_spec] * 3,
        out_specs=vmem_spec,
        compiler_params=pltpu.CompilerParams(vmem_limit_bytes=4 << 20),
        name="output",
    )(found, mine, new_kv, w_out, in_hbm(w_gate), in_hbm(w_up), in_hbm(w_down))

    here, there = pair_sum(partial_attn)
    down_part, mid = pl.pallas_call(
        feed_kernel,
        out_shape=(
            jax.ShapeDtypeStruct((count, model), BF16),
            jax.ShapeDtypeStruct((count, model), F32),
        ),
        compiler_params=pltpu.CompilerParams(vmem_limit_bytes=6 << 20),
        name="feed",
    )(tokens, here, there, ffn_gain.reshape(gain_shape), w_gate, w_up, w_down)

    here, there = pair_sum(down_part)
    hidden_out = mid + (here.astype(F32) + there.astype(F32))
    return (hidden_out, new_kv.reshape(count, 2, half))


def solution(mesh):
    placed = (
        P("req", None),
        P("req"),
        P(),
        P("req"),
        P("req"),
        P("req", None, "tp"),
        P(),
        P(None, "tp"),
        P(None, "tp"),
        P(None, "tp"),
        P("tp", None),
        P(),
        P(None, "tp"),
        P(None, "tp"),
        P("tp", None),
    )
    return jax.shard_map(
        per_device,
        mesh=mesh,
        in_specs=placed,
        out_specs=(P("req", None), P("req", None, "tp")),
        check_vma=False,
    )
```

```python
import math

import jax
import jax.numpy as jnp
import numpy as np
from jax import lax
from jax.experimental import pallas as pl
from jax.experimental.pallas import tpu as pltpu
from jax.sharding import PartitionSpec as P

HEAD_DIM = 128
ROPE_BASE = 1000000.0
EPS = 1e-05
FLOOR = -1e30
LOWEST = -1e29
LOG2E = 1.4426950408889634
TILE = 256
SUB = 128
WIN = 8
PIECES = 8
SLAB = 1024
F32 = jnp.float32
BF16 = jnp.bfloat16
VMEM = pltpu.VMEM


def mm(a, b, dims=((1,), (0,))):
    return lax.dot_general(a, b, (dims, ((), ())), preferred_element_type=F32)


def norm_rows(rows, gain_ref):
    mean_sq = jnp.mean(rows * rows, axis=-1, keepdims=True)
    scaled = rows * lax.rsqrt(mean_sq + EPS)
    gain = gain_ref[...].astype(F32)
    blocks = [
        scaled[:, i * HEAD_DIM : (i + 1) * HEAD_DIM] * gain[i : i + 1, :] for i in range(gain.shape[0])
    ]
    return jnp.concatenate(blocks, axis=1).astype(BF16)


def column(row_ref, count):
    shape = (count, count)
    diagonal = lax.broadcasted_iota(jnp.int32, shape, 0) == lax.broadcasted_iota(jnp.int32, shape, 1)
    values = jnp.broadcast_to(row_ref[...].astype(F32), shape)
    return jnp.sum(jnp.where(diagonal, values, 0.0), axis=1, keepdims=True)


def fetch(pairs, sems):
    copies = [pltpu.make_async_copy(src, dst, sems.at[i]) for i, (src, dst) in enumerate(pairs)]
    for copy in copies:
        copy.start()
    return copies


def project_kernel(
    tokens_hbm, gain_hbm, place_hbm, len_hbm, freq_hbm, order_hbm, wq_hbm,
    msg_ref, mine_ref, normed_hbm, turn_hbm, sort_hbm, upto_hbm, back_hbm,
    tokens, gain, place, lens, freq, order, wq, normed_ref, turn, sort_ref, upto_ref, back_ref, sems, out_sems,
):
    sources, count, wide = msg_ref.shape
    width = wide - HEAD_DIM
    rows = wq.shape[0] // PIECES
    small = [(tokens_hbm, tokens), (gain_hbm, gain), (place_hbm, place), (len_hbm, lens)]
    small += [(freq_hbm, freq), (order_hbm, order)]
    slabs = [pl.ds(i * rows, rows) for i in range(PIECES)]
    copies = fetch(small + [(wq_hbm.at[at, :], wq.at[at, :]) for at in slabs], sems)
    for copy in copies[: len(small)]:
        copy.wait()
    normed = norm_rows(tokens[...].astype(F32), gain)
    normed_ref[...] = normed
    lane = lax.broadcasted_iota(jnp.int32, (count, HEAD_DIM), 1)
    angle = column(place, count) * freq[...]
    cosine = jnp.cos(angle)
    sine = jnp.where(lane < HEAD_DIM // 2, -1.0, 1.0) * jnp.sin(angle)
    turn[0:count, :] = cosine
    turn[count:, :] = sine
    length = column(lens, count)
    high = jnp.floor(length * (1.0 / 128.0))
    coded = jnp.where(lane < HEAD_DIM // 2, high, length - 128.0 * high).astype(BF16)
    reqs = order.shape[1]
    row = lax.broadcasted_iota(jnp.int32, (reqs, reqs), 0)
    col = lax.broadcasted_iota(jnp.int32, (reqs, reqs), 1)
    sort = (column(order, reqs) == col.astype(F32)).astype(F32)
    sort_ref[...] = sort.astype(BF16)
    rank = jnp.sum(sort * row.astype(F32), axis=0, keepdims=True)
    upto_ref[...] = (rank <= row.astype(F32)).astype(F32).astype(BF16)
    back_ref[...] = (order[...] == row).astype(F32).astype(BF16)
    early = [(normed_ref, normed_hbm), (turn, turn_hbm), (sort_ref, sort_hbm), (upto_ref, upto_hbm), (back_ref, back_hbm)]
    outs = fetch(early, out_sems)
    q = jnp.zeros((count, width), F32)
    for copy, at in zip(copies[len(small) :], slabs):
        copy.wait()
        q = q + mm(normed[:, at.start : at.start + rows], wq[at, :])
    parts = []
    for low in range(0, width, HEAD_DIM):
        x = q[:, low : low + HEAD_DIM]
        parts.append((x * cosine + pltpu.roll(x, HEAD_DIM // 2, 1) * sine).astype(BF16))
    msg = jnp.concatenate(parts + [coded], axis=1)
    mine_ref[...] = msg
    for r in range(sources):
        msg_ref[r, :, :] = msg
    for out in outs:
        out.wait()


def prepare_kernel(
    normed_hbm, turn_hbm, wk_hbm, wv_hbm, cache_hbm,
    kv_ref, key_ref, near_ref, far_hbm,
    normed_ref, turn, wk, wv, cache, wide, far, sems, out_sems,
):
    half = wk.shape[1]
    slabs = cache.shape[0] // SLAB
    per_slot = 2 * half // HEAD_DIM
    spots = [pl.ds(i * SLAB, SLAB) for i in range(slabs)]
    wanted = [(cache_hbm.at[at, :], cache.at[at, :]) for at in spots]
    copies = fetch([(normed_hbm, normed_ref), (turn_hbm, turn), (wk_hbm, wk), (wv_hbm, wv)] + wanted, sems)
    for _ in range(3):
        copies.pop(0).wait()
    normed = normed_ref[...]
    cosine = turn[0 : turn.shape[0] // 2, :]
    sine = turn[turn.shape[0] // 2 :, :]
    k = mm(normed, wk[...])
    for low in range(0, half, HEAD_DIM):
        x = k[:, low : low + HEAD_DIM]
        kv_ref[:, low : low + HEAD_DIM] = x * cosine + pltpu.roll(x, HEAD_DIM // 2, 1) * sine
    copies.pop(0).wait()
    kv_ref[:, half:] = mm(normed, wv[...])
    slots = SLAB // per_slot
    outs = []
    for i, at in enumerate(spots):
        copies[i].wait()
        wide[i % 2, :, :] = cache[at, :].astype(F32)
        for j in range(per_slot):
            rows = wide[i % 2, pl.ds(j, slots, stride=per_slot), :].astype(BF16)
            to, first = key_ref, i * slots
            if j % 2:
                to, first = (far, first) if i < slabs // 2 else (near_ref, first - far.shape[0])
            to[first : first + slots, (j // 2) * HEAD_DIM : (j // 2 + 1) * HEAD_DIM] = rows
        if i < slabs // 2 and i % 4 == 3:
            block = pl.ds((i - 3) * slots, 4 * slots)
            outs.append(pltpu.make_async_copy(far.at[block, :], far_hbm.at[block, :], out_sems.at[i // 4]))
            outs[-1].start()
    for out in outs:
        out.wait()


def attend_kernel(
    base_ref, msg_ref, sort_ref, upto_ref, back_ref, live_ref, key_ref, near_ref, far_hbm, later_hbm,
    out_ref,
    queries, starts, ends, top, total, summed, held, weights, value_ref, ranks, ranks_s, sem, load_sems,
):
    middle = far_hbm.shape[0]
    loads = fetch(
        [
            (far_hbm, value_ref.at[pl.ds(0, middle), :]),
            (near_ref, value_ref.at[pl.ds(middle, middle), :]),
        ],
        load_sems,
    )
    reqs = msg_ref.shape[0]
    width = msg_ref.shape[1] - HEAD_DIM
    heads = width // HEAD_DIM
    group = heads // (key_ref.shape[1] // HEAD_DIM)
    tiles = key_ref.shape[0] // TILE
    factor = LOG2E / math.sqrt(HEAD_DIM)
    base = base_ref[0].astype(F32)

    lane = lax.broadcasted_iota(jnp.int32, (reqs, HEAD_DIM), 1)
    high_half = lane < HEAD_DIM // 2

    def joined(counts):
        turned = pltpu.roll(counts, HEAD_DIM // 2, 1)
        return jnp.where(high_half, 128.0 * counts + turned, counts + 128.0 * turned)

    upto = joined(mm(upto_ref[...], msg_ref[:, width:])) - base
    edge = (lane * TILE).astype(F32)
    first = jnp.sum((upto <= edge).astype(F32), axis=0, keepdims=True).astype(jnp.int32)
    begins = [first[0, t] for t in range(tiles + 1)]
    widest = begins[1] - begins[0]
    for t in range(1, tiles):
        widest = jnp.maximum(widest, begins[t + 1] - begins[t])
    ranks[0:1, :] = first
    sorted_q = mm(sort_ref[...], msg_ref[:, :width])
    far = jnp.full((WIN, HEAD_DIM), 1e9, F32)
    ends[0:reqs, :] = upto
    ends[reqs:, :] = far
    row = lax.broadcasted_iota(jnp.int32, (reqs, HEAD_DIM), 0)
    starts[0:reqs, :] = jnp.where(row == 0, -base, pltpu.roll(upto, 1, 0))
    starts[reqs:, :] = far
    for h in range(heads):
        queries[h, 0:reqs, :] = sorted_q[:, h * HEAD_DIM : (h + 1) * HEAD_DIM]
        queries[h, reqs:, :] = jnp.zeros((WIN, HEAD_DIM), F32)
    top[...] = jnp.full(top.shape, LOWEST, F32)
    total[...] = jnp.zeros(total.shape, F32)
    summed[...] = jnp.zeros(summed.shape, F32)

    def spot(h, rank):
        return (h, pl.ds(rank, WIN), slice(None))

    def of_head(x, h):
        return x[h * WIN : (h + 1) * WIN, :]

    def masked_scores(tile, rank):
        none = jnp.zeros((WIN, HEAD_DIM), BF16)
        lines = []
        for h in range(heads):
            q = queries[spot(h, rank)].astype(BF16)
            lines.append(
                jnp.concatenate([q if c == h // group else none for c in range(heads // group)], axis=1)
            )
        keys = key_ref[pl.ds(tile * TILE, TILE), :]
        scores = mm(jnp.concatenate(lines, axis=0), keys, ((1,), (1,))) * factor
        low = starts[pl.ds(rank, WIN), :]
        high = ends[pl.ds(rank, WIN), :]
        masks = []
        for i in range(TILE // SUB):
            block = tile * (TILE // SUB) + i
            at = (lax.broadcasted_iota(jnp.int32, (1, SUB), 1) + block * SUB).astype(F32)
            at = jnp.where(live_ref[pl.ds(block, 1), :] == 1, at, -1e9)
            masks.append((at >= low) & (at < high))
        mask = jnp.concatenate(masks, axis=1)
        return jnp.concatenate([jnp.where(mask, of_head(scores, h), FLOOR) for h in range(heads)], axis=0)

    def values_of(tile, weight):
        value = mm(weight, value_ref[pl.ds(tile * TILE, TILE), :])
        return [
            of_head(value, h)[:, (h // group) * HEAD_DIM : (h // group + 1) * HEAD_DIM] for h in range(heads)
        ]

    for t in range(tiles):
        held[t, :, :] = masked_scores(t, begins[t])
    peaks = [jnp.max(held[t, :, :], axis=1, keepdims=True) for t in range(tiles)]
    for t in range(tiles):
        for h in range(heads):
            at = spot(h, begins[t])
            top[at] = jnp.maximum(top[at], of_head(peaks[t], h))
    counts = []
    for t in range(tiles):
        peak = jnp.concatenate([top[spot(h, begins[t])] for h in range(heads)], axis=0)
        weight = jnp.exp2(held[t, :, :] - jnp.concatenate([peak] * (TILE // HEAD_DIM), axis=1))
        weights[t, :, :] = weight.astype(BF16)
        counts.append(jnp.sum(weight, axis=1, keepdims=True))
    loads[0].wait()
    loads[1].wait()
    found = [values_of(t, weights[t, :, :]) for t in range(tiles)]
    for t in range(tiles):
        for h in range(heads):
            at = spot(h, begins[t])
            total[at] = total[at] + of_head(counts[t], h)
            summed[at] = summed[at] + found[t][h]

    def more(t, carry):
        begin = ranks_s[0, t]

        def again(i, inner):
            rank = begin + (i + 1) * WIN
            masked = masked_scores(t, rank)
            peak = jnp.maximum(jnp.max(masked, axis=1, keepdims=True), LOWEST)
            weight = jnp.exp2(masked - peak)
            count = jnp.sum(weight, axis=1, keepdims=True)
            value = values_of(t, weight.astype(BF16))
            for h in range(heads):
                at = spot(h, rank)
                old = top[at]
                new = jnp.maximum(old, of_head(peak, h))
                left = jnp.exp2(old - new)
                right = jnp.exp2(of_head(peak, h) - new)
                top[at] = new
                total[at] = total[at] * left + of_head(count, h) * right
                summed[at] = summed[at] * left + value[h] * right
            return inner

        return lax.fori_loop(0, (ranks_s[0, t + 1] - begin) // WIN, again, carry)

    @pl.when(widest >= WIN)
    def _():
        copy = pltpu.make_async_copy(ranks, ranks_s, sem)
        copy.start()
        copy.wait()
        lax.fori_loop(0, tiles, more, 0)

    columns = []
    sums = jnp.ones((reqs, HEAD_DIM), F32)
    peaks = jnp.zeros((reqs, HEAD_DIM), F32)
    for h in range(heads):
        count = total[h, 0:reqs, :]
        columns.append((summed[h, 0:reqs, :] / jnp.where(count > 0.0, count, 1.0)).astype(BF16))
        sums = jnp.where(lane % heads == h, count, sums)
        peaks = jnp.where(lane % heads == h, top[h, 0:reqs, :], peaks)
    some = sums > 0.0
    rest = jnp.where(some, peaks + jnp.log2(jnp.where(some, sums, 1.0)), LOWEST)
    extra = jnp.zeros((reqs, HEAD_DIM), F32)
    for piece in range(3):
        coded = rest.astype(BF16).astype(F32)
        extra = jnp.where(lane // heads == piece, coded, extra)
        rest = rest - coded
    both = jnp.concatenate(columns + [extra.astype(BF16)], axis=1)
    out_ref[...] = mm(back_ref[...], both).astype(BF16)


def output_kernel(parts_ref, msg_ref, kv_ref, w_ref, *rest):
    out_ref = rest[-1]
    sources, count, wide = parts_ref.shape
    width = wide - HEAD_DIM
    heads = width // HEAD_DIM
    half = kv_ref.shape[1] // 2
    group = heads // (half // HEAD_DIM)
    factor = LOG2E / math.sqrt(HEAD_DIM)
    levels = []
    for r in range(sources):
        e = parts_ref[r, :, width:].astype(F32)
        levels.append(
            e + (pltpu.roll(e, HEAD_DIM - heads, 1) + pltpu.roll(e, HEAD_DIM - 2 * heads, 1))
        )
    context = []
    for h in range(heads):
        at = slice(h * HEAD_DIM, (h + 1) * HEAD_DIM)
        low = (h // group) * HEAD_DIM
        key = kv_ref[:, low : low + HEAD_DIM].astype(BF16).astype(F32)
        value = kv_ref[:, half + low : half + low + HEAD_DIM].astype(BF16).astype(F32)
        own = jnp.sum(msg_ref[:, at].astype(F32) * key, axis=1, keepdims=True) * factor
        cols = [level[:, h : h + 1] for level in levels]
        peak = own
        for c in cols:
            peak = jnp.maximum(peak, c)
        weight = jnp.exp2(own - peak)
        denom = weight
        numer = weight * value
        for r in range(sources):
            weight = jnp.exp2(cols[r] - peak)
            denom = denom + weight
            numer = numer + weight * parts_ref[r, :, at].astype(F32)
        context.append((numer / denom).astype(BF16))
    out_ref[...] = mm(jnp.concatenate(context, axis=1), w_ref[...]).astype(BF16)


def feed_kernel(tokens_ref, here_ref, there_ref, gain_ref, wg_ref, wu_ref, wd_ref, part_ref, mid_ref):
    mid = tokens_ref[...].astype(F32) + (here_ref[...].astype(F32) + there_ref[...].astype(F32))
    mid_ref[...] = mid
    normed = norm_rows(mid, gain_ref)
    gate = mm(normed, wg_ref[...])
    upper = mm(normed, wu_ref[...])
    act = (gate / (1.0 + jnp.exp(-gate)) * upper).astype(BF16)
    part_ref[...] = mm(act, wd_ref[...]).astype(BF16)


def swap(x, axis, distance):
    return lax.ppermute(x, axis, [(i, i ^ distance) for i in range(lax.axis_size(axis))])


def pair_sum(x):
    size = lax.axis_size("tp")
    distance = 1
    while 2 * distance < size - 1:
        x = (x.astype(F32) + swap(x, "tp", distance).astype(F32)).astype(BF16)
        distance = 2 * distance + 1
    return x, swap(x, "tp", distance)


def in_hbm(x):
    return pltpu.with_memory_space_constraint(x, pltpu.HBM)


def in_vmem(x):
    return pltpu.with_memory_space_constraint(x, VMEM)


def per_device(
    tokens, lengths, pool_order, positions, slot_mask, kv_cache, attn_gain,
    w_query, w_key, w_value, w_out, ffn_gain, w_gate, w_up, w_down,
):
    count, model = tokens.shape
    nreq = lax.axis_size("req")
    reqs = count * nreq
    slot_count = kv_cache.shape[0]
    width = w_query.shape[1]
    half = w_key.shape[1]
    kv_heads = half // HEAD_DIM
    wide = width + HEAD_DIM
    assert slot_count % TILE == 0 and slot_count // TILE < HEAD_DIM

    hbm_spec = pl.BlockSpec(memory_space=pltpu.HBM)
    vmem_spec = pl.BlockSpec(memory_space=VMEM)
    pair = np.arange(HEAD_DIM) % (HEAD_DIM // 2)
    freq = jnp.asarray((ROPE_BASE ** (-(pair * 2.0) / HEAD_DIM)).astype(np.float32)).reshape(1, HEAD_DIM)
    gain_shape = (model // HEAD_DIM, HEAD_DIM)

    sizes = [((count, model), BF16), ((2 * count, HEAD_DIM), F32)]
    sizes += [((reqs, reqs), BF16)] * 3
    msg, mine, normed, turn, sort, upto, back = pl.pallas_call(
        project_kernel,
        out_shape=[jax.ShapeDtypeStruct((nreq, count, wide), BF16), VMEM((count, wide), BF16)]
        + [pltpu.HBM(*size) for size in sizes],
        in_specs=[hbm_spec] * 7,
        out_specs=[vmem_spec] * 2 + [hbm_spec] * 5,
        scratch_shapes=[
            VMEM((count, model), BF16),
            VMEM(gain_shape, BF16),
            VMEM((1, count), jnp.int32),
            VMEM((1, count), jnp.int32),
            VMEM((1, HEAD_DIM), F32),
            VMEM((1, reqs), jnp.int32),
            VMEM((model, width), BF16),
        ]
        + [VMEM(*size) for size in sizes]
        + [pltpu.SemaphoreType.DMA((6 + PIECES,)), pltpu.SemaphoreType.DMA((5,))],
        compiler_params=pltpu.CompilerParams(vmem_limit_bytes=(4 + (reqs // 128) ** 2) << 20),
        cost_estimate=pl.CostEstimate(flops=2 * count * model * width, bytes_accessed=3 * model * width, transcendentals=0),
        name="project",
    )(
        in_hbm(tokens),
        in_hbm(attn_gain.reshape(gain_shape)),
        in_hbm(positions.reshape(1, count)),
        in_hbm(lengths.reshape(1, count)),
        in_hbm(freq),
        in_hbm(pool_order.reshape(1, reqs)),
        in_hbm(w_query),
    )

    everyone = lax.all_to_all(msg, "req", 0, 0).reshape(reqs, wide)

    cache = kv_cache.reshape(slot_count, 2, kv_heads, HEAD_DIM).transpose(0, 2, 1, 3)
    cache = cache.reshape(slot_count * 2 * kv_heads, HEAD_DIM)
    new_kv, keys, near, far = pl.pallas_call(
        prepare_kernel,
        out_shape=(
            VMEM((count, 2 * half), F32),
            VMEM((slot_count, half), BF16),
            VMEM((slot_count // 2, half), BF16),
            pltpu.HBM((slot_count // 2, half), BF16),
        ),
        in_specs=[hbm_spec] * 5,
        out_specs=[vmem_spec, vmem_spec, vmem_spec, hbm_spec],
        scratch_shapes=[
            VMEM((count, model), BF16),
            VMEM((2 * count, HEAD_DIM), F32),
            VMEM((model, half), BF16),
            VMEM((model, half), BF16),
            VMEM(cache.shape, BF16),
            VMEM((2, SLAB, HEAD_DIM), F32),
            VMEM((slot_count // 2, half), BF16),
            pltpu.SemaphoreType.DMA((cache.shape[0] // SLAB + 4,)),
            pltpu.SemaphoreType.DMA((cache.shape[0] // SLAB // 8,)),
        ],
        compiler_params=pltpu.CompilerParams(vmem_limit_bytes=12 << 20),
        cost_estimate=pl.CostEstimate(flops=4 * count * model * half, bytes_accessed=3 * cache.size, transcendentals=0),
        name="prepare",
    )(in_hbm(normed), in_hbm(turn), in_hbm(w_key), in_hbm(w_value), in_hbm(cache))

    live = slot_mask.reshape(slot_count // SUB, SUB)
    base = (lax.axis_index("req") * slot_count).astype(jnp.int32).reshape(1)
    rows = reqs + WIN
    heads = width // HEAD_DIM
    tiles = slot_count // TILE
    per_head = (heads, rows, HEAD_DIM)
    parts = pl.pallas_call(
        attend_kernel,
        out_shape=jax.ShapeDtypeStruct((reqs, wide), BF16),
        in_specs=[pl.BlockSpec(memory_space=pltpu.SMEM)] + [vmem_spec] * 7 + [hbm_spec] * 2,
        out_specs=vmem_spec,
        scratch_shapes=[
            VMEM(per_head, F32),
            VMEM((rows, HEAD_DIM), F32),
            VMEM((rows, HEAD_DIM), F32),
            VMEM(per_head, F32),
            VMEM(per_head, F32),
            VMEM(per_head, F32),
            VMEM((tiles, heads * WIN, TILE), F32),
            VMEM((tiles, heads * WIN, TILE), BF16),
            VMEM((slot_count, half), BF16),
            VMEM((8, HEAD_DIM), jnp.int32),
            pltpu.SMEM((8, HEAD_DIM), jnp.int32),
            pltpu.SemaphoreType.DMA,
            pltpu.SemaphoreType.DMA((2,)),
        ],
        compiler_params=pltpu.CompilerParams(vmem_limit_bytes=(4 + reqs // 32) << 20),
        cost_estimate=pl.CostEstimate(flops=1 << 30, bytes_accessed=8 << 20, transcendentals=0),
        name="attend",
    )(base, everyone, sort, upto, back, live, keys, near, in_hbm(far), in_hbm(w_gate))

    found = lax.all_to_all(parts.reshape(nreq, count, wide), "req", 0, 0)

    partial_attn = pl.pallas_call(
        output_kernel,
        out_shape=jax.ShapeDtypeStruct((count, model), BF16),
        in_specs=[vmem_spec] * 4 + [hbm_spec] * 3,
        out_specs=vmem_spec,
        compiler_params=pltpu.CompilerParams(vmem_limit_bytes=4 << 20),
        name="output",
    )(found, mine, new_kv, w_out, in_hbm(w_gate), in_hbm(w_up), in_hbm(w_down))

    here, there = pair_sum(partial_attn)
    down_part, mid = pl.pallas_call(
        feed_kernel,
        out_shape=(
            jax.ShapeDtypeStruct((count, model), BF16),
            jax.ShapeDtypeStruct((count, model), F32),
        ),
        compiler_params=pltpu.CompilerParams(vmem_limit_bytes=6 << 20),
        name="feed",
    )(tokens, here, there, ffn_gain.reshape(gain_shape), w_gate, w_up, w_down)

    here, there = pair_sum(down_part)
    hidden_out = mid + (here.astype(F32) + there.astype(F32))
    return (hidden_out, new_kv.reshape(count, 2, half))


def solution(mesh):
    placed = (
        P("req", None),
        P("req"),
        P(),
        P("req"),
        P("req"),
        P("req", None, "tp"),
        P(),
        P(None, "tp"),
        P(None, "tp"),
        P(None, "tp"),
        P("tp", None),
        P(),
        P(None, "tp"),
        P(None, "tp"),
        P("tp", None),
    )
    return jax.shard_map(
        per_device,
        mesh=mesh,
        in_specs=placed,
        out_specs=(P("req", None), P("req", None, "tp")),
        check_vma=False,
    )
```

```python
import math

import jax
import jax.numpy as jnp
import numpy as np
from jax import lax
from jax.experimental import pallas as pl
from jax.experimental.pallas import tpu as pltpu
from jax.sharding import PartitionSpec as P

HEAD_DIM = 128
ROPE_BASE = 1000000.0
EPS = 1e-05
FLOOR = -1e30
LOWEST = -1e29
LOG2E = 1.4426950408889634
TILE = 256
SUB = 128
WIN = 8
PIECES = 8
SLAB = 1024
F32 = jnp.float32
BF16 = jnp.bfloat16
VMEM = pltpu.VMEM


def mm(a, b, dims=((1,), (0,))):
    return lax.dot_general(a, b, (dims, ((), ())), preferred_element_type=F32)


def norm_rows(rows, gain_ref):
    mean_sq = jnp.mean(rows * rows, axis=-1, keepdims=True)
    scaled = rows * lax.rsqrt(mean_sq + EPS)
    gain = gain_ref[...].astype(F32)
    blocks = [
        scaled[:, i * HEAD_DIM : (i + 1) * HEAD_DIM] * gain[i : i + 1, :] for i in range(gain.shape[0])
    ]
    return jnp.concatenate(blocks, axis=1).astype(BF16)


def column(row_ref, count):
    shape = (count, count)
    diagonal = lax.broadcasted_iota(jnp.int32, shape, 0) == lax.broadcasted_iota(jnp.int32, shape, 1)
    values = jnp.broadcast_to(row_ref[...].astype(F32), shape)
    return jnp.sum(jnp.where(diagonal, values, 0.0), axis=1, keepdims=True)


def fetch(pairs, sems):
    copies = [pltpu.make_async_copy(src, dst, sems.at[i]) for i, (src, dst) in enumerate(pairs)]
    for copy in copies:
        copy.start()
    return copies


def project_kernel(
    tokens_hbm, gain_hbm, place_hbm, len_hbm, freq_hbm, order_hbm, wq_hbm,
    msg_ref, mine_ref, normed_hbm, turn_hbm, sort_hbm, upto_hbm, back_hbm,
    tokens, gain, place, lens, freq, order, wq, normed_ref, turn, sort_ref, upto_ref, back_ref, sems, out_sems,
):
    sources, count, wide = msg_ref.shape
    width = wide - HEAD_DIM
    rows = wq.shape[0] // PIECES
    small = [(tokens_hbm, tokens), (gain_hbm, gain), (place_hbm, place), (len_hbm, lens)]
    small += [(freq_hbm, freq), (order_hbm, order)]
    slabs = [pl.ds(i * rows, rows) for i in range(PIECES)]
    copies = fetch(small + [(wq_hbm.at[at, :], wq.at[at, :]) for at in slabs], sems)
    for copy in copies[: len(small)]:
        copy.wait()
    normed = norm_rows(tokens[...].astype(F32), gain)
    normed_ref[...] = normed
    lane = lax.broadcasted_iota(jnp.int32, (count, HEAD_DIM), 1)
    angle = column(place, count) * freq[...]
    cosine = jnp.cos(angle)
    sine = jnp.where(lane < HEAD_DIM // 2, -1.0, 1.0) * jnp.sin(angle)
    turn[0:count, :] = cosine
    turn[count:, :] = sine
    length = column(lens, count)
    high = jnp.floor(length * (1.0 / 128.0))
    coded = jnp.where(lane < HEAD_DIM // 2, high, length - 128.0 * high).astype(BF16)
    reqs = order.shape[1]
    row = lax.broadcasted_iota(jnp.int32, (reqs, reqs), 0)
    col = lax.broadcasted_iota(jnp.int32, (reqs, reqs), 1)
    sort = (column(order, reqs) == col.astype(F32)).astype(F32)
    sort_ref[...] = sort.astype(BF16)
    rank = jnp.sum(sort * row.astype(F32), axis=0, keepdims=True)
    upto_ref[...] = (rank <= row.astype(F32)).astype(F32).astype(BF16)
    back_ref[...] = (order[...] == row).astype(F32).astype(BF16)
    early = [(normed_ref, normed_hbm), (turn, turn_hbm), (sort_ref, sort_hbm), (upto_ref, upto_hbm), (back_ref, back_hbm)]
    outs = fetch(early, out_sems)
    q = jnp.zeros((count, width), F32)
    for copy, at in zip(copies[len(small) :], slabs):
        copy.wait()
        q = q + mm(normed[:, at.start : at.start + rows], wq[at, :])
    parts = []
    for low in range(0, width, HEAD_DIM):
        x = q[:, low : low + HEAD_DIM]
        parts.append((x * cosine + pltpu.roll(x, HEAD_DIM // 2, 1) * sine).astype(BF16))
    msg = jnp.concatenate(parts + [coded], axis=1)
    mine_ref[...] = msg
    for r in range(sources):
        msg_ref[r, :, :] = msg
    for out in outs:
        out.wait()


def prepare_kernel(
    normed_hbm, turn_hbm, wk_hbm, wv_hbm, cache_hbm,
    kv_ref, key_ref, near_ref, far_hbm,
    normed_ref, turn, wk, wv, cache, wide, far, sems, out_sems,
):
    half = wk.shape[1]
    slabs = cache.shape[0] // SLAB
    per_slot = 2 * half // HEAD_DIM
    spots = [pl.ds(i * SLAB, SLAB) for i in range(slabs)]
    wanted = [(cache_hbm.at[at, :], cache.at[at, :]) for at in spots]
    copies = fetch([(normed_hbm, normed_ref), (turn_hbm, turn), (wk_hbm, wk), (wv_hbm, wv)] + wanted, sems)
    for _ in range(3):
        copies.pop(0).wait()
    normed = normed_ref[...]
    cosine = turn[0 : turn.shape[0] // 2, :]
    sine = turn[turn.shape[0] // 2 :, :]
    k = mm(normed, wk[...])
    for low in range(0, half, HEAD_DIM):
        x = k[:, low : low + HEAD_DIM]
        kv_ref[:, low : low + HEAD_DIM] = x * cosine + pltpu.roll(x, HEAD_DIM // 2, 1) * sine
    copies.pop(0).wait()
    kv_ref[:, half:] = mm(normed, wv[...])
    slots = SLAB // per_slot
    outs = []
    for i, at in enumerate(spots):
        copies[i].wait()
        wide[i % 2, :, :] = cache[at, :].astype(F32)
        for j in range(per_slot):
            rows = wide[i % 2, pl.ds(j, slots, stride=per_slot), :].astype(BF16)
            to, first = key_ref, i * slots
            if j % 2:
                to, first = (far, first) if i < slabs // 2 else (near_ref, first - far.shape[0])
            to[first : first + slots, (j // 2) * HEAD_DIM : (j // 2 + 1) * HEAD_DIM] = rows
        if i < slabs // 2 and i % 4 == 3:
            block = pl.ds((i - 3) * slots, 4 * slots)
            outs.append(pltpu.make_async_copy(far.at[block, :], far_hbm.at[block, :], out_sems.at[i // 4]))
            outs[-1].start()
    for out in outs:
        out.wait()


def attend_kernel(
    base_ref, msg_ref, sort_ref, upto_ref, back_ref, live_ref, key_ref, near_ref, far_hbm, later_hbm,
    out_ref,
    queries, starts, ends, top, total, summed, held, weights, value_ref, ranks, ranks_s, sem, load_sems,
):
    middle = far_hbm.shape[0]
    loads = fetch(
        [
            (far_hbm, value_ref.at[pl.ds(0, middle), :]),
            (near_ref, value_ref.at[pl.ds(middle, middle), :]),
        ],
        load_sems,
    )
    reqs = msg_ref.shape[0]
    width = msg_ref.shape[1] - HEAD_DIM
    heads = width // HEAD_DIM
    group = heads // (key_ref.shape[1] // HEAD_DIM)
    tiles = key_ref.shape[0] // TILE
    factor = LOG2E / math.sqrt(HEAD_DIM)
    base = base_ref[0].astype(F32)

    lane = lax.broadcasted_iota(jnp.int32, (reqs, HEAD_DIM), 1)
    high_half = lane < HEAD_DIM // 2

    def joined(counts):
        turned = pltpu.roll(counts, HEAD_DIM // 2, 1)
        return jnp.where(high_half, 128.0 * counts + turned, counts + 128.0 * turned)

    upto = joined(mm(upto_ref[...], msg_ref[:, width:])) - base
    edge = (lane * TILE).astype(F32)
    first = jnp.sum((upto <= edge).astype(F32), axis=0, keepdims=True).astype(jnp.int32)
    begins = [first[0, t] for t in range(tiles + 1)]
    widest = begins[1] - begins[0]
    for t in range(1, tiles):
        widest = jnp.maximum(widest, begins[t + 1] - begins[t])
    ranks[0:1, :] = first
    sorted_q = mm(sort_ref[...], msg_ref[:, :width])
    far = jnp.full((WIN, HEAD_DIM), 1e9, F32)
    ends[0:reqs, :] = upto
    ends[reqs:, :] = far
    row = lax.broadcasted_iota(jnp.int32, (reqs, HEAD_DIM), 0)
    starts[0:reqs, :] = jnp.where(row == 0, -base, pltpu.roll(upto, 1, 0))
    starts[reqs:, :] = far
    for h in range(heads):
        queries[h, 0:reqs, :] = sorted_q[:, h * HEAD_DIM : (h + 1) * HEAD_DIM]
        queries[h, reqs:, :] = jnp.zeros((WIN, HEAD_DIM), F32)
    top[...] = jnp.full(top.shape, LOWEST, F32)
    total[...] = jnp.zeros(total.shape, F32)
    summed[...] = jnp.zeros(summed.shape, F32)

    def spot(h, rank):
        return (h, pl.ds(rank, WIN), slice(None))

    def of_head(x, h):
        return x[h * WIN : (h + 1) * WIN, :]

    def masked_scores(tile, rank):
        none = jnp.zeros((WIN, HEAD_DIM), BF16)
        lines = []
        for h in range(heads):
            q = queries[spot(h, rank)].astype(BF16)
            lines.append(
                jnp.concatenate([q if c == h // group else none for c in range(heads // group)], axis=1)
            )
        keys = key_ref[pl.ds(tile * TILE, TILE), :]
        scores = mm(jnp.concatenate(lines, axis=0), keys, ((1,), (1,))) * factor
        low = starts[pl.ds(rank, WIN), :]
        high = ends[pl.ds(rank, WIN), :]
        masks = []
        for i in range(TILE // SUB):
            block = tile * (TILE // SUB) + i
            at = (lax.broadcasted_iota(jnp.int32, (1, SUB), 1) + block * SUB).astype(F32)
            at = jnp.where(live_ref[pl.ds(block, 1), :] == 1, at, -1e9)
            masks.append((at >= low) & (at < high))
        mask = jnp.concatenate(masks, axis=1)
        return jnp.concatenate([jnp.where(mask, of_head(scores, h), FLOOR) for h in range(heads)], axis=0)

    def values_of(tile, weight):
        value = mm(weight, value_ref[pl.ds(tile * TILE, TILE), :])
        return [
            of_head(value, h)[:, (h // group) * HEAD_DIM : (h // group + 1) * HEAD_DIM] for h in range(heads)
        ]

    for t in range(tiles):
        held[t, :, :] = masked_scores(t, begins[t])
    peaks = [jnp.max(held[t, :, :], axis=1, keepdims=True) for t in range(tiles)]
    for t in range(tiles):
        for h in range(heads):
            at = spot(h, begins[t])
            top[at] = jnp.maximum(top[at], of_head(peaks[t], h))
    counts = []
    for t in range(tiles):
        peak = jnp.concatenate([top[spot(h, begins[t])] for h in range(heads)], axis=0)
        weight = jnp.exp2(held[t, :, :] - jnp.concatenate([peak] * (TILE // HEAD_DIM), axis=1))
        weights[t, :, :] = weight.astype(BF16)
        counts.append(jnp.sum(weight, axis=1, keepdims=True))
    loads[0].wait()
    loads[1].wait()
    found = [values_of(t, weights[t, :, :]) for t in range(tiles)]
    for t in range(tiles):
        for h in range(heads):
            at = spot(h, begins[t])
            total[at] = total[at] + of_head(counts[t], h)
            summed[at] = summed[at] + found[t][h]

    def more(t, carry):
        begin = ranks_s[0, t]

        def again(i, inner):
            rank = begin + (i + 1) * WIN
            masked = masked_scores(t, rank)
            peak = jnp.maximum(jnp.max(masked, axis=1, keepdims=True), LOWEST)
            weight = jnp.exp2(masked - peak)
            count = jnp.sum(weight, axis=1, keepdims=True)
            value = values_of(t, weight.astype(BF16))
            for h in range(heads):
                at = spot(h, rank)
                old = top[at]
                new = jnp.maximum(old, of_head(peak, h))
                left = jnp.exp2(old - new)
                right = jnp.exp2(of_head(peak, h) - new)
                top[at] = new
                total[at] = total[at] * left + of_head(count, h) * right
                summed[at] = summed[at] * left + value[h] * right
            return inner

        return lax.fori_loop(0, (ranks_s[0, t + 1] - begin) // WIN, again, carry)

    @pl.when(widest >= WIN)
    def _():
        copy = pltpu.make_async_copy(ranks, ranks_s, sem)
        copy.start()
        copy.wait()
        lax.fori_loop(0, tiles, more, 0)

    columns = []
    sums = jnp.ones((reqs, HEAD_DIM), F32)
    peaks = jnp.zeros((reqs, HEAD_DIM), F32)
    for h in range(heads):
        count = total[h, 0:reqs, :]
        columns.append((summed[h, 0:reqs, :] / jnp.where(count > 0.0, count, 1.0)).astype(BF16))
        sums = jnp.where(lane % heads == h, count, sums)
        peaks = jnp.where(lane % heads == h, top[h, 0:reqs, :], peaks)
    some = sums > 0.0
    rest = jnp.where(some, peaks + jnp.log2(jnp.where(some, sums, 1.0)), LOWEST)
    extra = jnp.zeros((reqs, HEAD_DIM), F32)
    for piece in range(3):
        coded = rest.astype(BF16).astype(F32)
        extra = jnp.where(lane // heads == piece, coded, extra)
        rest = rest - coded
    both = jnp.concatenate(columns + [extra.astype(BF16)], axis=1)
    out_ref[...] = mm(back_ref[...], both).astype(BF16)


def output_kernel(parts_ref, msg_ref, kv_ref, w_ref, *rest):
    out_ref = rest[-1]
    sources, count, wide = parts_ref.shape
    width = wide - HEAD_DIM
    heads = width // HEAD_DIM
    half = kv_ref.shape[1] // 2
    group = heads // (half // HEAD_DIM)
    factor = LOG2E / math.sqrt(HEAD_DIM)
    levels = []
    for r in range(sources):
        e = parts_ref[r, :, width:].astype(F32)
        levels.append(
            e + (pltpu.roll(e, HEAD_DIM - heads, 1) + pltpu.roll(e, HEAD_DIM - 2 * heads, 1))
        )
    context = []
    for h in range(heads):
        at = slice(h * HEAD_DIM, (h + 1) * HEAD_DIM)
        low = (h // group) * HEAD_DIM
        key = kv_ref[:, low : low + HEAD_DIM].astype(BF16).astype(F32)
        value = kv_ref[:, half + low : half + low + HEAD_DIM].astype(BF16).astype(F32)
        own = jnp.sum(msg_ref[:, at].astype(F32) * key, axis=1, keepdims=True) * factor
        cols = [level[:, h : h + 1] for level in levels]
        peak = own
        for c in cols:
            peak = jnp.maximum(peak, c)
        weight = jnp.exp2(own - peak)
        denom = weight
        numer = weight * value
        for r in range(sources):
            weight = jnp.exp2(cols[r] - peak)
            denom = denom + weight
            numer = numer + weight * parts_ref[r, :, at].astype(F32)
        context.append((numer / denom).astype(BF16))
    out_ref[...] = mm(jnp.concatenate(context, axis=1), w_ref[...]).astype(BF16)


def feed_kernel(tokens_ref, here_ref, there_ref, gain_ref, wg_ref, wu_ref, wd_ref, part_ref, mid_ref):
    mid = tokens_ref[...].astype(F32) + (here_ref[...].astype(F32) + there_ref[...].astype(F32))
    mid_ref[...] = mid
    normed = norm_rows(mid, gain_ref)
    act = []
    for low in range(0, wg_ref.shape[1], TILE):
        gate = mm(normed, wg_ref[:, low : low + TILE])
        upper = mm(normed, wu_ref[:, low : low + TILE])
        act.append((gate / (1.0 + jnp.exp(-gate)) * upper).astype(BF16))
    part_ref[...] = mm(jnp.concatenate(act, axis=1), wd_ref[...]).astype(BF16)


def swap(x, axis, distance):
    return lax.ppermute(x, axis, [(i, i ^ distance) for i in range(lax.axis_size(axis))])


def pair_sum(x):
    size = lax.axis_size("tp")
    distance = 1
    while 2 * distance < size - 1:
        x = (x.astype(F32) + swap(x, "tp", distance).astype(F32)).astype(BF16)
        distance = 2 * distance + 1
    return x, swap(x, "tp", distance)


def in_hbm(x):
    return pltpu.with_memory_space_constraint(x, pltpu.HBM)


def in_vmem(x):
    return pltpu.with_memory_space_constraint(x, VMEM)


def per_device(
    tokens, lengths, pool_order, positions, slot_mask, kv_cache, attn_gain,
    w_query, w_key, w_value, w_out, ffn_gain, w_gate, w_up, w_down,
):
    count, model = tokens.shape
    nreq = lax.axis_size("req")
    reqs = count * nreq
    slot_count = kv_cache.shape[0]
    width = w_query.shape[1]
    half = w_key.shape[1]
    kv_heads = half // HEAD_DIM
    wide = width + HEAD_DIM
    assert slot_count % TILE == 0 and slot_count // TILE < HEAD_DIM

    hbm_spec = pl.BlockSpec(memory_space=pltpu.HBM)
    vmem_spec = pl.BlockSpec(memory_space=VMEM)
    pair = np.arange(HEAD_DIM) % (HEAD_DIM // 2)
    freq = jnp.asarray((ROPE_BASE ** (-(pair * 2.0) / HEAD_DIM)).astype(np.float32)).reshape(1, HEAD_DIM)
    gain_shape = (model // HEAD_DIM, HEAD_DIM)

    sizes = [((count, model), BF16), ((2 * count, HEAD_DIM), F32)]
    sizes += [((reqs, reqs), BF16)] * 3
    msg, mine, normed, turn, sort, upto, back = pl.pallas_call(
        project_kernel,
        out_shape=[jax.ShapeDtypeStruct((nreq, count, wide), BF16), VMEM((count, wide), BF16)]
        + [pltpu.HBM(*size) for size in sizes],
        in_specs=[hbm_spec] * 7,
        out_specs=[vmem_spec] * 2 + [hbm_spec] * 5,
        scratch_shapes=[
            VMEM((count, model), BF16),
            VMEM(gain_shape, BF16),
            VMEM((1, count), jnp.int32),
            VMEM((1, count), jnp.int32),
            VMEM((1, HEAD_DIM), F32),
            VMEM((1, reqs), jnp.int32),
            VMEM((model, width), BF16),
        ]
        + [VMEM(*size) for size in sizes]
        + [pltpu.SemaphoreType.DMA((6 + PIECES,)), pltpu.SemaphoreType.DMA((5,))],
        compiler_params=pltpu.CompilerParams(vmem_limit_bytes=(4 + (reqs // 128) ** 2) << 20),
        cost_estimate=pl.CostEstimate(flops=2 * count * model * width, bytes_accessed=3 * model * width, transcendentals=0),
        name="project",
    )(
        in_hbm(tokens),
        in_hbm(attn_gain.reshape(gain_shape)),
        in_hbm(positions.reshape(1, count)),
        in_hbm(lengths.reshape(1, count)),
        in_hbm(freq),
        in_hbm(pool_order.reshape(1, reqs)),
        in_hbm(w_query),
    )

    everyone = lax.all_to_all(msg, "req", 0, 0).reshape(reqs, wide)

    cache = kv_cache.reshape(slot_count, 2, kv_heads, HEAD_DIM).transpose(0, 2, 1, 3)
    cache = cache.reshape(slot_count * 2 * kv_heads, HEAD_DIM)
    new_kv, keys, near, far = pl.pallas_call(
        prepare_kernel,
        out_shape=(
            VMEM((count, 2 * half), F32),
            VMEM((slot_count, half), BF16),
            VMEM((slot_count // 2, half), BF16),
            pltpu.HBM((slot_count // 2, half), BF16),
        ),
        in_specs=[hbm_spec] * 5,
        out_specs=[vmem_spec, vmem_spec, vmem_spec, hbm_spec],
        scratch_shapes=[
            VMEM((count, model), BF16),
            VMEM((2 * count, HEAD_DIM), F32),
            VMEM((model, half), BF16),
            VMEM((model, half), BF16),
            VMEM(cache.shape, BF16),
            VMEM((2, SLAB, HEAD_DIM), F32),
            VMEM((slot_count // 2, half), BF16),
            pltpu.SemaphoreType.DMA((cache.shape[0] // SLAB + 4,)),
            pltpu.SemaphoreType.DMA((cache.shape[0] // SLAB // 8,)),
        ],
        compiler_params=pltpu.CompilerParams(vmem_limit_bytes=12 << 20),
        cost_estimate=pl.CostEstimate(flops=4 * count * model * half, bytes_accessed=3 * cache.size, transcendentals=0),
        name="prepare",
    )(in_hbm(normed), in_hbm(turn), in_hbm(w_key), in_hbm(w_value), in_hbm(cache))

    live = slot_mask.reshape(slot_count // SUB, SUB)
    base = (lax.axis_index("req") * slot_count).astype(jnp.int32).reshape(1)
    rows = reqs + WIN
    heads = width // HEAD_DIM
    tiles = slot_count // TILE
    per_head = (heads, rows, HEAD_DIM)
    parts = pl.pallas_call(
        attend_kernel,
        out_shape=jax.ShapeDtypeStruct((reqs, wide), BF16),
        in_specs=[pl.BlockSpec(memory_space=pltpu.SMEM)] + [vmem_spec] * 7 + [hbm_spec] * 2,
        out_specs=vmem_spec,
        scratch_shapes=[
            VMEM(per_head, F32),
            VMEM((rows, HEAD_DIM), F32),
            VMEM((rows, HEAD_DIM), F32),
            VMEM(per_head, F32),
            VMEM(per_head, F32),
            VMEM(per_head, F32),
            VMEM((tiles, heads * WIN, TILE), F32),
            VMEM((tiles, heads * WIN, TILE), BF16),
            VMEM((slot_count, half), BF16),
            VMEM((8, HEAD_DIM), jnp.int32),
            pltpu.SMEM((8, HEAD_DIM), jnp.int32),
            pltpu.SemaphoreType.DMA,
            pltpu.SemaphoreType.DMA((2,)),
        ],
        compiler_params=pltpu.CompilerParams(vmem_limit_bytes=(4 + reqs // 32) << 20),
        cost_estimate=pl.CostEstimate(flops=1 << 30, bytes_accessed=8 << 20, transcendentals=0),
        name="attend",
    )(base, everyone, sort, upto, back, live, keys, near, in_hbm(far), in_hbm(w_gate))

    found = lax.all_to_all(parts.reshape(nreq, count, wide), "req", 0, 0)

    partial_attn = pl.pallas_call(
        output_kernel,
        out_shape=jax.ShapeDtypeStruct((count, model), BF16),
        in_specs=[vmem_spec] * 4 + [hbm_spec] * 3,
        out_specs=vmem_spec,
        compiler_params=pltpu.CompilerParams(vmem_limit_bytes=4 << 20),
        name="output",
    )(found, mine, new_kv, w_out, in_hbm(w_gate), in_hbm(w_up), in_hbm(w_down))

    here, there = pair_sum(partial_attn)
    down_part, mid = pl.pallas_call(
        feed_kernel,
        out_shape=(
            jax.ShapeDtypeStruct((count, model), BF16),
            jax.ShapeDtypeStruct((count, model), F32),
        ),
        compiler_params=pltpu.CompilerParams(vmem_limit_bytes=6 << 20),
        name="feed",
    )(tokens, here, there, ffn_gain.reshape(gain_shape), w_gate, w_up, w_down)

    here, there = pair_sum(down_part)
    hidden_out = mid + (here.astype(F32) + there.astype(F32))
    return (hidden_out, new_kv.reshape(count, 2, half))


def solution(mesh):
    placed = (
        P("req", None),
        P("req"),
        P(),
        P("req"),
        P("req"),
        P("req", None, "tp"),
        P(),
        P(None, "tp"),
        P(None, "tp"),
        P(None, "tp"),
        P("tp", None),
        P(),
        P(None, "tp"),
        P(None, "tp"),
        P("tp", None),
    )
    return jax.shard_map(
        per_device,
        mesh=mesh,
        in_specs=placed,
        out_specs=(P("req", None), P("req", None, "tp")),
        check_vma=False,
    )
```
